32 devices in a mesh: space: 4 (over z), bal: 8 (over y, x, core).
Axes of the slice: x: 2, y: 2, z: 4, core: 2. Of those that a mesh axis runs over, the one named last changes fastest.
Arguments:
- panels: bfloat16 [4, 8, 1024, 1024], P('space', 'bal'), may hold values from -0.1875 to 0.1875
- enrich: int32 [4, 8], P('space', 'bal'), may hold values from 1 to 2
- compliance: float32 [4, 8, 1024], P('space', 'bal'), may hold values from 0.5 to 2
- loads: float32 [4, 8, 64, 1024], P('space', 'bal'), may hold values from -6 to 6
- face_maps: int32 [4, 8, 4, 256], P('space', 'bal'), may hold values from 0 to 255, each once within a row
- face_lengths: int32 [4, 8, 4], P('space', 'bal'), may hold values from 128 to 256, as said below
- contact: int32 [4, 8, 128], P('space', 'bal'), may hold values from 0 to 1023
Outputs:
- solution: float32 [4, 8, 64, 1024], P('space', 'bal')
- residual: float32 [4, 8, 64, 1024], P('space', 'bal')
- violation: float32 [64], replicated
The draws below stay inside these ranges and needn't reach their ends.
Inputs may be any that keep to these rules, and one draw needn't show every extreme that they name: `face_maps`: each face's slot-to-row table is a permutation of its 256 rows. `face_lengths`: the two faces of one shared interface have the same length; some face has all 256 slots live.
All inputs are finite; a program needn't handle non-finite values.
Results may differ from the reference program's by a relative error of at most 0.0003.
Values sent between devices are 32-bit elements; how exact they have to be, the bound alone decides.
A program may use at most 64 MiB of HBM per device.

```python
import math
import jax
import jax.numpy as jnp
from jax import lax

IFACE = 1024
FACE = 256
ROWS = 1024
BLOCK_ROWS = 512
LOADS = 64
ITERS = 3
CONTACT = 128
SUB_S = 4
SUB_B = 8


def draw_face_lengths(key, part):
    first_key, second_key = jax.random.split(jax.random.fold_in(key, 11))
    shortest = FACE // 2
    space_len = jax.random.randint(first_key, (SUB_S + 1, SUB_B), shortest, FACE + 1).astype(jnp.int32)
    space_len = space_len.at[1, 0].set(FACE)
    bal_len = jax.random.randint(second_key, (SUB_S, SUB_B + 1), shortest, FACE + 1).astype(jnp.int32)
    stacked = jnp.stack([space_len[:-1], space_len[1:], bal_len[:, :-1], bal_len[:, 1:]], axis=2)
    return stacked.astype(jnp.int32)


def plant(drawn, rng, least, largest):
    extent = drawn.shape
    spot = [jax.random.randint(jax.random.fold_in(rng, axis), (), 0, extent[axis]) for axis in range(len(extent))]
    drawn = drawn.at[tuple(spot)].set(least)
    longest = extent.index(max(extent))
    spot[longest] = (spot[longest] + 1) % extent[longest]
    return drawn.at[tuple(spot)].set(largest)


def levels(rng, shape, pieces, low, top_value):
    def one(dim, parts):
        heights = jax.random.uniform(jax.random.fold_in(jax.random.fold_in(rng, 6), dim), (parts,), jnp.float32, low / len(pieces), top_value / len(pieces))
        return jnp.repeat(jnp.exp(heights), shape[dim] // parts).reshape((-1,) + (1,) * (len(shape) - dim - 1))

    gain = one(*pieces[0])
    for cut in pieces[1:]:
        gain = gain * one(*cut)
    return gain


def centred(stream_key, extent, scale, reach, pieces=(), kind=jnp.bfloat16):
    level = levels(stream_key, extent, pieces, -0.22, 0.18) if pieces else 1.0
    drawn = jax.random.normal(stream_key, extent, jnp.float32) * scale * level
    return jnp.minimum(jnp.maximum(drawn, -reach), reach).astype(kind)


def setup_inputs(seed: int = 0) -> dict:
    arg_keys = jax.random.split(jax.random.key(seed), 8)
    panels = centred(arg_keys[0], (SUB_S, SUB_B, ROWS, IFACE), ROWS ** -0.5, 0.1875, ((0, 4), (1, 8)))
    enrich = plant(jax.random.randint(arg_keys[1], (SUB_S, SUB_B), 1, ROWS // BLOCK_ROWS + 1), jax.random.fold_in(arg_keys[1], 1), 1, (ROWS // BLOCK_ROWS + 1) - 1).astype(jnp.int32)
    compliance = jnp.clip(jnp.exp(math.log(2.0) - 1.3862944 * jax.random.uniform(arg_keys[2], (SUB_S, SUB_B, IFACE), jnp.float32) ** levels(arg_keys[2], (SUB_S, SUB_B, IFACE), ((0, 4), (1, 8)), -0.2, 0.2)), 0.5, 2.0)
    loads = centred(arg_keys[3], (SUB_S, SUB_B, LOADS, IFACE), 1.0, 6.0, ((0, 4), (1, 8)), jnp.float32)
    face_maps = jax.vmap(lambda own: jax.random.permutation(own, FACE))(jax.random.split(arg_keys[4], SUB_S * SUB_B * 4)).reshape((SUB_S, SUB_B, 4, FACE)).astype(jnp.int32)
    face_lengths = draw_face_lengths(jax.random.fold_in(arg_keys[7], 71), 0)
    contact = plant(jax.random.randint(arg_keys[6], (SUB_S, SUB_B, CONTACT), 0, IFACE), jax.random.fold_in(arg_keys[6], 1), 0, IFACE - 1).astype(jnp.int32)
    return dict(panels=panels, enrich=enrich, compliance=compliance, loads=loads, face_maps=face_maps, face_lengths=face_lengths, contact=contact)


def chebyshev_constants():
    upper = 2.6 * (1.0 + math.sqrt(IFACE / ROWS)) ** 2 + 4.0
    lower = 0.5
    center = (upper + lower) / 2.0
    half_span = (upper - lower) / 2.0
    return (center, half_span, center / half_span)

def apply_local(direction, panels, enrich, compliance):
    row_index = jnp.arange(ROWS, dtype=jnp.int32)

    def one_sub(member):
        load_rows, panel_rows, live_blocks, diag_terms = member
        row_keep = (row_index < live_blocks * BLOCK_ROWS).astype(jnp.float32)
        kept = panel_rows.astype(jnp.float32) * row_keep[:, None]
        projected = jnp.dot(load_rows, kept.T, precision=lax.Precision.HIGHEST)
        return jnp.dot(projected, kept, precision=lax.Precision.HIGHEST) + load_rows * diag_terms[None, :]
    applied = lax.map(one_sub, (direction.reshape(-1, LOADS, IFACE), panels.reshape(-1, ROWS, IFACE), enrich.reshape(-1), compliance.reshape(-1, IFACE)))
    return applied.reshape(direction.shape)

def assemble_all(values, position, back_position):
    canonical = jnp.take_along_axis(values, jnp.broadcast_to(position, values.shape), axis=3)
    canonical = canonical.reshape(SUB_S, SUB_B, LOADS, 4, IFACE // 4)
    zero_space = jnp.zeros_like(canonical[:1, :, :, 0])
    zero_bal = jnp.zeros_like(canonical[:, :1, :, 0])
    from_below = jnp.concatenate([zero_space, canonical[:-1, :, :, 1]], axis=0)
    from_above = jnp.concatenate([canonical[1:, :, :, 0], zero_space], axis=0)
    from_left = jnp.concatenate([zero_bal, canonical[:, :-1, :, 3]], axis=1)
    from_right = jnp.concatenate([canonical[:, 1:, :, 2], zero_bal], axis=1)
    summed = canonical + jnp.stack([from_below, from_above, from_left, from_right], axis=3)
    summed = summed.reshape(values.shape)
    return jnp.take_along_axis(summed, jnp.broadcast_to(back_position, values.shape), axis=3)

def reference(panels, enrich, compliance, loads, face_maps, face_lengths, contact):
    face_len = IFACE // 4
    canon_slot = jnp.arange(face_len, dtype=jnp.int32)
    live_canon = (canon_slot[None, None, None, :] < face_lengths[:, :, :, None]).astype(jnp.float32)
    inverse = jnp.argsort(face_maps, axis=3).astype(jnp.int32)
    live_local = jnp.take_along_axis(live_canon, inverse, axis=3).reshape(SUB_S, SUB_B, 1, IFACE)
    offsets = (jnp.arange(4, dtype=jnp.int32) * face_len)[None, None, :, None]
    position = (face_maps + offsets).astype(jnp.int32).reshape(SUB_S, SUB_B, 1, IFACE)
    back_position = (inverse + offsets).astype(jnp.int32).reshape(SUB_S, SUB_B, 1, IFACE)
    center, half_span, ratio_c = chebyshev_constants()
    residual = assemble_all(live_local * loads, position, back_position)
    direction = residual / center
    solution = jnp.zeros_like(residual)
    cheb_rho = 1.0 / ratio_c
    for iteration in range(ITERS):
        solution = solution + direction
        image = live_local * apply_local(direction, panels, enrich, compliance)
        residual = residual - assemble_all(image, position, back_position)
        if iteration + 1 < ITERS:
            rho_next = 1.0 / (2.0 * ratio_c - cheb_rho)
            direction = rho_next * cheb_rho * direction + 2.0 * rho_next / half_span * residual
            cheb_rho = rho_next
    contact_index = jnp.broadcast_to(contact[:, :, None, :], (SUB_S, SUB_B, LOADS, CONTACT))
    gathered = jnp.take_along_axis(solution, contact_index, axis=3)
    negative = jnp.minimum(gathered, 0.0)
    violation = jnp.sqrt(lax.optimization_barrier(jnp.sum(negative * negative, axis=(0, 1, 3))) + 1e-06)
    return (solution, residual, violation)
```

```python
import functools
import math

import jax
import jax.numpy as jnp
from jax import lax
from jax.experimental import pallas as pl
from jax.experimental.pallas import tpu as pltpu
from jax.sharding import PartitionSpec as P

BLOCK_ROWS = 512
ITERS = 3
FACES = 4
SEND_ORDER = (0, 1, 2, 3)
WAIT_ORDER = (2, 3, 0, 1)
MESH = pl.DeviceIdType.MESH
CONTRACT_LAST = (((1,), (1,)), ((), ()))
CONTRACT_MIDDLE = (((1,), (0,)), ((), ()))


def chebyshev_constants(iface, rows):
    upper = 2.6 * (1.0 + math.sqrt(iface / rows)) ** 2 + 4.0
    lower = 0.5
    center = (upper + lower) / 2.0
    half_span = (upper - lower) / 2.0
    return (center, half_span, center / half_span)


def parts(value, count):
    taken = []
    rest = value
    for index in range(count):
        part = rest.astype(jnp.bfloat16)
        taken.append(part)
        if index + 1 < count:
            rest = rest - part.astype(jnp.float32)
    return jnp.concatenate(taken, axis=0)


def product(value, matrix, dims, count=2):
    rows = value.shape[0]
    stacked = lax.dot_general(
        parts(value, count), matrix, dims, preferred_element_type=jnp.float32
    )
    total = stacked[:rows]
    for index in range(1, count):
        total = total + stacked[index * rows : (index + 1) * rows]
    return total


def kernel(
    n_space, n_bal,
    lengths_ref, enrich_ref, maps_ref, compliance_ref, contact_ref, loads_ref, panel_hbm,
    solution_ref, residual_ref, violation_ref,
    panel, kept, onehot, diag, direction, total, residual, send, recv, bal_sums, space_sums, own_bal, own_space,
    panel_sem, send_sem, recv_sem, bal_send, bal_recv, space_send, space_recv,
):
    me_s = lax.axis_index("space")
    me_b = lax.axis_index("bal")
    rows, columns = panel.shape
    face_len = columns // FACES
    loads = loads_ref.shape[0]
    center, half_span, ratio_c = chebyshev_constants(columns, rows)

    panel_copy = pltpu.make_async_copy(panel_hbm, panel, panel_sem)
    panel_copy.start()

    barrier = pltpu.get_barrier_semaphore()
    for step in range(1, n_bal):
        pl.semaphore_signal(
            barrier, inc=1, device_id={"bal": lax.rem(me_b + step, n_bal)}, device_id_type=MESH
        )
    for step in range(1, n_space):
        pl.semaphore_signal(
            barrier, inc=1, device_id={"space": lax.rem(me_s + step, n_space)}, device_id_type=MESH
        )

    present = (me_s > 0, me_s < n_space - 1, me_b > 0, me_b < n_bal - 1)
    across = (
        {"space": jnp.maximum(me_s - 1, 0)},
        {"space": jnp.minimum(me_s + 1, n_space - 1)},
        {"bal": jnp.maximum(me_b - 1, 0)},
        {"bal": jnp.minimum(me_b + 1, n_bal - 1)},
    )

    def face_copy(turn, face):
        return pltpu.make_async_remote_copy(
            src_ref=send.at[turn, face],
            dst_ref=recv.at[turn, face ^ 1],
            send_sem=send_sem.at[turn, face],
            recv_sem=recv_sem.at[turn, face ^ 1],
            device_id=across[face],
            device_id_type=MESH,
        )

    def start_face(turn, face):
        @pl.when(present[face])
        def _():
            face_copy(turn, face).start()

    def wait_face(turn, face):
        @pl.when(present[face])
        def _():
            face_copy(turn, face ^ 1).wait_recv()

    def span(face):
        return slice(face * face_len, (face + 1) * face_len)

    row_of = lax.broadcasted_iota(jnp.int32, (face_len, face_len), 0)
    slot_of = lax.broadcasted_iota(jnp.int32, (face_len, face_len), 1)
    for face in range(FACES):
        table = jnp.broadcast_to(maps_ref[face : face + 1, :], (face_len, face_len))
        hit = (row_of == table) & (slot_of < lengths_ref[0, face])
        onehot[face] = jnp.where(hit, 1.0, 0.0).astype(jnp.bfloat16)

    for face in SEND_ORDER:
        send[0, face] = product(loads_ref[:, span(face)], onehot[face], CONTRACT_MIDDLE)

    pl.semaphore_wait(barrier, n_bal - 1 + n_space - 1)
    for face in SEND_ORDER:
        start_face(0, face)

    for face in range(FACES):
        @pl.when(jnp.logical_not(present[face]))
        def _():
            for turn in range(ITERS + 1):
                recv[turn, face] = jnp.zeros((loads, face_len), jnp.float32)

    for face in range(FACES):
        wide = jnp.broadcast_to(compliance_ref[:, span(face)], (16, face_len))
        diag[:, span(face)] = product(wide, onehot[face], CONTRACT_MIDDLE, 3)

    lane = 128
    contact = contact_ref[...]
    groups = columns // lane
    group_rows = max(groups, 8)
    group_of = lax.broadcasted_iota(jnp.int32, (group_rows, contact.shape[1]), 0)
    place_of = lax.broadcasted_iota(jnp.int32, (lane, contact.shape[1]), 0)
    in_group = jnp.where(group_of == lax.shift_right_logical(contact, 7), 1.0, 0.0)
    at_place = jnp.where(place_of == (contact & (lane - 1)), 1.0, 0.0)
    counts = lax.dot_general(
        in_group.astype(jnp.bfloat16), at_place.astype(jnp.bfloat16), CONTRACT_LAST,
        preferred_element_type=jnp.float32,
    )

    panel_copy.wait()
    live_rows = enrich_ref[0, 0] * BLOCK_ROWS
    keep = lax.broadcasted_iota(jnp.int32, (rows, face_len), 0) < live_rows
    for face in range(FACES):
        picked = jnp.dot(panel[:, span(face)], onehot[face], preferred_element_type=jnp.float32)
        kept[:, span(face)] = jnp.where(keep, picked, 0.0).astype(jnp.bfloat16)

    def project(face, running):
        term = lax.dot_general(
            parts(direction[:, span(face)], 2), kept[:, span(face)], CONTRACT_LAST,
            preferred_element_type=jnp.float32,
        )
        return term if running is None else running + term

    running = None
    for face in WAIT_ORDER:
        wait_face(0, face)
        first = send[0, face] + recv[0, face]
        residual[:, span(face)] = first
        direction[:, span(face)] = first / center
        total[:, span(face)] = first / center
        running = project(face, running)

    cheb_rho = 1.0 / ratio_c
    for iteration in range(ITERS):
        turn = iteration + 1
        last = turn == ITERS
        if last:
            weighted = jnp.zeros((loads, lane), jnp.float32)
            for face in range(FACES):
                local = product(total[:, span(face)], onehot[face], CONTRACT_LAST)
                solution_ref[:, span(face)] = local
                negative = jnp.minimum(local, 0.0)
                squares = negative * negative
                for piece in range(face_len // lane):
                    group = face * (face_len // lane) + piece
                    weighted = weighted + squares[:, piece * lane : (piece + 1) * lane] * counts[group : group + 1, :]
            pieces = parts(weighted, 3)
            ones = jnp.ones((16, lane), jnp.bfloat16)
            spread = lax.dot_general(ones, pieces, CONTRACT_LAST, preferred_element_type=jnp.float32)
            terms = spread[:8, :loads] + spread[:8, loads : 2 * loads] + spread[:8, 2 * loads :]
            own_bal[:, :loads] = terms
            own_bal[:, loads:] = jnp.zeros((8, own_bal.shape[1] - loads), jnp.float32)
            bal_sums[me_b] = own_bal[...]
            for step in range(1, n_bal):
                pltpu.make_async_remote_copy(
                    src_ref=own_bal, dst_ref=bal_sums.at[me_b],
                    send_sem=bal_send.at[step], recv_sem=bal_recv.at[step],
                    device_id={"bal": lax.rem(me_b + step, n_bal)}, device_id_type=MESH,
                ).start()

        projected = parts(running[:loads] + running[loads:], 2)
        for face in SEND_ORDER:
            stacked = jnp.dot(projected, kept[:, span(face)], preferred_element_type=jnp.float32)
            send[turn, face] = (
                stacked[:loads] + stacked[loads:] + direction[:, span(face)] * diag[0:1, span(face)]
            )
            start_face(turn, face)

        if last:
            for step in range(1, n_bal):
                source = lax.rem(me_b + n_bal - step, n_bal)
                pltpu.make_async_remote_copy(
                    src_ref=own_bal, dst_ref=bal_sums.at[source],
                    send_sem=bal_send.at[step], recv_sem=bal_recv.at[step],
                    device_id={"bal": source}, device_id_type=MESH,
                ).wait()
            summed = bal_sums[0]
            for index in range(1, n_bal):
                summed = summed + bal_sums[index]
            own_space[...] = summed
            space_sums[me_s] = summed
            for step in range(1, n_space):
                pltpu.make_async_remote_copy(
                    src_ref=own_space, dst_ref=space_sums.at[me_s],
                    send_sem=space_send.at[step], recv_sem=space_recv.at[step],
                    device_id={"space": lax.rem(me_s + step, n_space)}, device_id_type=MESH,
                ).start()
            for face in WAIT_ORDER:
                wait_face(turn, face)
                final = residual[:, span(face)] - (send[turn, face] + recv[turn, face])
                residual_ref[:, span(face)] = product(final, onehot[face], CONTRACT_LAST)
        else:
            rho_next = 1.0 / (2.0 * ratio_c - cheb_rho)
            running = None
            for face in WAIT_ORDER:
                wait_face(turn, face)
                updated = residual[:, span(face)] - (send[turn, face] + recv[turn, face])
                residual[:, span(face)] = updated
                moved = rho_next * cheb_rho * direction[:, span(face)] + 2.0 * rho_next / half_span * updated
                direction[:, span(face)] = moved
                total[:, span(face)] = total[:, span(face)] + moved
                running = project(face, running)
            cheb_rho = rho_next

    for step in range(1, n_space):
        source = lax.rem(me_s + n_space - step, n_space)
        pltpu.make_async_remote_copy(
            src_ref=own_space, dst_ref=space_sums.at[source],
            send_sem=space_send.at[step], recv_sem=space_recv.at[step],
            device_id={"space": source}, device_id_type=MESH,
        ).wait()
    summed = space_sums[0]
    for index in range(1, n_space):
        summed = summed + space_sums[index]
    violation_ref[...] = jnp.sqrt(summed[0:1, :loads] + 1e-06)

    for turn in range(ITERS + 1):
        for face in range(FACES):
            @pl.when(present[face])
            def _():
                face_copy(turn, face).wait_send()


def local(n_space, n_bal, panels, enrich, compliance, loads, face_maps, face_lengths, contact):
    rows, columns = panels.shape[2:]
    n_loads = loads.shape[2]
    face_len = columns // FACES
    width = -(-n_loads // 128) * 128
    vmem = pl.BlockSpec(memory_space=pltpu.VMEM)
    smem = pl.BlockSpec(memory_space=pltpu.SMEM)
    turns = ITERS + 1
    flops = 2 * rows * columns * (face_len + ITERS * 4 * n_loads)
    field = (n_loads, columns)
    out = pl.pallas_call(
        functools.partial(kernel, n_space, n_bal),
        out_shape=(
            jax.ShapeDtypeStruct(field, jnp.float32),
            jax.ShapeDtypeStruct(field, jnp.float32),
            jax.ShapeDtypeStruct((1, n_loads), jnp.float32),
        ),
        in_specs=[smem, smem, vmem, vmem, vmem, vmem, pl.BlockSpec(memory_space=pl.ANY)],
        out_specs=(vmem, vmem, vmem),
        scratch_shapes=[
            pltpu.VMEM((rows, columns), jnp.bfloat16),
            pltpu.VMEM((rows, columns), jnp.bfloat16),
            pltpu.VMEM((FACES, face_len, face_len), jnp.bfloat16),
            pltpu.VMEM((16, columns), jnp.float32),
            pltpu.VMEM(field, jnp.float32),
            pltpu.VMEM(field, jnp.float32),
            pltpu.VMEM(field, jnp.float32),
            pltpu.VMEM((turns, FACES, n_loads, face_len), jnp.float32),
            pltpu.VMEM((turns, FACES, n_loads, face_len), jnp.float32),
            pltpu.VMEM((n_bal, 8, width), jnp.float32),
            pltpu.VMEM((n_space, 8, width), jnp.float32),
            pltpu.VMEM((8, width), jnp.float32),
            pltpu.VMEM((8, width), jnp.float32),
            pltpu.SemaphoreType.DMA,
            pltpu.SemaphoreType.DMA((turns, FACES)),
            pltpu.SemaphoreType.DMA((turns, FACES)),
            pltpu.SemaphoreType.DMA((n_bal,)),
            pltpu.SemaphoreType.DMA((n_bal,)),
            pltpu.SemaphoreType.DMA((n_space,)),
            pltpu.SemaphoreType.DMA((n_space,)),
        ],
        compiler_params=pltpu.CompilerParams(
            collective_id=0, has_side_effects=True, vmem_limit_bytes=48 * 1024 * 1024
        ),
        cost_estimate=pl.CostEstimate(
            flops=flops, bytes_accessed=2 * rows * columns + 12 * n_loads * columns, transcendentals=n_loads
        ),
        name="feti",
    )(
        face_lengths[0], enrich, face_maps[0, 0], compliance[0], contact[0], loads[0, 0], panels[0, 0]
    )
    return (out[0][None, None], out[1][None, None], out[2][0])


def solution(mesh):
    in_specs = (
        P("space", "bal", None, None),
        P("space", "bal"),
        P("space", "bal", None),
        P("space", "bal", None, None),
        P("space", "bal", None, None),
        P("space", "bal", None),
        P("space", "bal", None),
    )
    out_specs = (P("space", "bal", None, None), P("space", "bal", None, None), P())
    body = functools.partial(local, mesh.shape["space"], mesh.shape["bal"])
    return jax.shard_map(body, mesh=mesh, in_specs=in_specs, out_specs=out_specs, check_vma=False)
```

```python
import functools
import math

import jax
import jax.numpy as jnp
from jax import lax
from jax.experimental import pallas as pl
from jax.experimental.pallas import tpu as pltpu
from jax.sharding import PartitionSpec as P

BLOCK_ROWS = 512
ITERS = 3
FACES = 4
VMEM_BYTES = 64 * 1024 * 1024
SEND_ORDER = (0, 1, 2, 3)
WAIT_ORDER = (2, 3, 0, 1)
MESH = pl.DeviceIdType.MESH
CONTRACT_LAST = (((1,), (1,)), ((), ()))
CONTRACT_MIDDLE = (((1,), (0,)), ((), ()))


def chebyshev_constants(iface, rows):
    upper = 2.6 * (1.0 + math.sqrt(iface / rows)) ** 2 + 4.0
    lower = 0.5
    center = (upper + lower) / 2.0
    half_span = (upper - lower) / 2.0
    return (center, half_span, center / half_span)


def parts(value, count):
    taken = []
    rest = value
    for index in range(count):
        part = rest.astype(jnp.bfloat16)
        taken.append(part)
        if index + 1 < count:
            rest = rest - part.astype(jnp.float32)
    return jnp.concatenate(taken, axis=0)


def product(value, matrix, dims, count=2):
    rows = value.shape[0]
    stacked = lax.dot_general(
        parts(value, count), matrix, dims, preferred_element_type=jnp.float32
    )
    total = stacked[:rows]
    for index in range(1, count):
        total = total + stacked[index * rows : (index + 1) * rows]
    return total


def kernel(
    n_space, n_bal,
    lengths_hbm, enrich_ref, maps_hbm, compliance_hbm, contact_hbm, loads_hbm, panel_hbm,
    solution_hbm, residual_hbm, violation_hbm,
    lengths_ref, maps_ref, compliance_ref, contact_ref, loads_ref,
    solution_ref, residual_ref, violation_ref, turned, panel, kept, kept_turned, onehot, diag, direction, total, residual, send, recv, bal_sums, space_sums, own_bal, own_space,
    input_sem, output_sem, send_sem, recv_sem, bal_send, bal_recv, space_send, space_recv,
):
    me_s = lax.axis_index("space")
    me_b = lax.axis_index("bal")
    rows, columns = panel.shape
    face_len = columns // FACES
    loads = loads_ref.shape[0]
    center, half_span, ratio_c = chebyshev_constants(columns, rows)

    inputs = (
        (maps_hbm, maps_ref), (lengths_hbm, lengths_ref), (loads_hbm, loads_ref), (panel_hbm, panel),
        (compliance_hbm, compliance_ref), (contact_hbm, contact_ref),
    )
    copies = [
        pltpu.make_async_copy(source, target, input_sem.at[index])
        for index, (source, target) in enumerate(inputs)
    ]
    for copy in copies:
        copy.start()

    barrier = pltpu.get_barrier_semaphore()
    for step in range(1, n_bal):
        pl.semaphore_signal(
            barrier, inc=1, device_id={"bal": lax.rem(me_b + step, n_bal)}, device_id_type=MESH
        )
    for step in range(1, n_space):
        pl.semaphore_signal(
            barrier, inc=1, device_id={"space": lax.rem(me_s + step, n_space)}, device_id_type=MESH
        )

    present = (me_s > 0, me_s < n_space - 1, me_b > 0, me_b < n_bal - 1)
    across = (
        {"space": jnp.maximum(me_s - 1, 0)},
        {"space": jnp.minimum(me_s + 1, n_space - 1)},
        {"bal": jnp.maximum(me_b - 1, 0)},
        {"bal": jnp.minimum(me_b + 1, n_bal - 1)},
    )

    def face_copy(turn, face):
        return pltpu.make_async_remote_copy(
            src_ref=send.at[turn, face],
            dst_ref=recv.at[turn, face ^ 1],
            send_sem=send_sem.at[turn, face],
            recv_sem=recv_sem.at[turn, face ^ 1],
            device_id=across[face],
            device_id_type=MESH,
        )

    def start_face(turn, face):
        @pl.when(present[face])
        def _():
            face_copy(turn, face).start()

    def wait_face(turn, face):
        @pl.when(present[face])
        def _():
            face_copy(turn, face ^ 1).wait_recv()

    def span(face):
        return slice(face * face_len, (face + 1) * face_len)

    copies[0].wait()
    copies[1].wait()
    row_of = lax.broadcasted_iota(jnp.int32, (face_len, face_len), 0)
    slot_of = lax.broadcasted_iota(jnp.int32, (face_len, face_len), 1)
    for face in range(FACES):
        table = jnp.broadcast_to(maps_ref[face : face + 1, :], (face_len, face_len))
        hit = (row_of == table) & (slot_of < lengths_ref[0, face])
        onehot[face] = jnp.where(hit, 1.0, 0.0).astype(jnp.bfloat16)

    copies[2].wait()
    for face in SEND_ORDER:
        send[0, face] = product(loads_ref[:, span(face)], onehot[face], CONTRACT_MIDDLE)

    pl.semaphore_wait(barrier, n_bal - 1 + n_space - 1)
    for face in SEND_ORDER:
        start_face(0, face)

    for face in range(FACES):
        @pl.when(jnp.logical_not(present[face]))
        def _():
            for turn in range(ITERS + 1):
                recv[turn, face] = jnp.zeros((loads, face_len), jnp.float32)

    for index in range(4, len(copies)):
        copies[index].wait()
    for face in range(FACES):
        turned[face] = onehot[face].T
        wide = jnp.broadcast_to(compliance_ref[:, span(face)], (16, face_len))
        diag[:, span(face)] = product(wide, onehot[face], CONTRACT_MIDDLE, 3)

    lane = 128
    contact = contact_ref[...]
    groups = columns // lane
    group_rows = max(groups, 8)
    group_of = lax.broadcasted_iota(jnp.int32, (group_rows, contact.shape[1]), 0)
    place_of = lax.broadcasted_iota(jnp.int32, (lane, contact.shape[1]), 0)
    in_group = jnp.where(group_of == lax.shift_right_logical(contact, 7), 1.0, 0.0)
    at_place = jnp.where(place_of == (contact & (lane - 1)), 1.0, 0.0)
    counts = lax.dot_general(
        in_group.astype(jnp.bfloat16), at_place.astype(jnp.bfloat16), CONTRACT_LAST,
        preferred_element_type=jnp.float32,
    )

    copies[3].wait()
    live_rows = enrich_ref[0, 0] * BLOCK_ROWS
    keep = lax.broadcasted_iota(jnp.int32, (rows, face_len), 0) < live_rows
    for face in range(FACES):
        picked = jnp.dot(panel[:, span(face)], onehot[face], preferred_element_type=jnp.float32)
        masked = jnp.where(keep, picked, 0.0).astype(jnp.bfloat16)
        kept[:, span(face)] = masked
        kept_turned[span(face), :] = masked.T

    def project(face, running):
        term = jnp.dot(
            parts(direction[:, span(face)], 2), kept_turned[span(face), :], preferred_element_type=jnp.float32
        )
        return term if running is None else running + term

    running = None
    for face in WAIT_ORDER:
        wait_face(0, face)
        first = send[0, face] + recv[0, face]
        residual[:, span(face)] = first
        direction[:, span(face)] = first / center
        total[:, span(face)] = first / center
        running = project(face, running)

    cheb_rho = 1.0 / ratio_c
    for iteration in range(ITERS):
        turn = iteration + 1
        last = turn == ITERS
        if last:
            weighted = jnp.zeros((loads, lane), jnp.float32)
            for face in range(FACES):
                local = product(total[:, span(face)], turned[face], CONTRACT_MIDDLE)
                solution_ref[:, span(face)] = local
                negative = jnp.minimum(local, 0.0)
                squares = negative * negative
                for piece in range(face_len // lane):
                    group = face * (face_len // lane) + piece
                    weighted = weighted + squares[:, piece * lane : (piece + 1) * lane] * counts[group : group + 1, :]
            pieces = parts(weighted, 3)
            ones = jnp.ones((16, lane), jnp.bfloat16)
            spread = lax.dot_general(ones, pieces, CONTRACT_LAST, preferred_element_type=jnp.float32)
            terms = spread[:8, :loads] + spread[:8, loads : 2 * loads] + spread[:8, 2 * loads :]
            own_bal[:, :loads] = terms
            own_bal[:, loads:] = jnp.zeros((8, own_bal.shape[1] - loads), jnp.float32)
            bal_sums[me_b] = own_bal[...]
            for step in range(1, n_bal):
                pltpu.make_async_remote_copy(
                    src_ref=own_bal, dst_ref=bal_sums.at[me_b],
                    send_sem=bal_send.at[step], recv_sem=bal_recv.at[step],
                    device_id={"bal": lax.rem(me_b + step, n_bal)}, device_id_type=MESH,
                ).start()

        projected = parts(running[:loads] + running[loads:], 2)
        for face in SEND_ORDER:
            stacked = jnp.dot(projected, kept[:, span(face)], preferred_element_type=jnp.float32)
            send[turn, face] = (
                stacked[:loads] + stacked[loads:] + direction[:, span(face)] * diag[0:1, span(face)]
            )
            start_face(turn, face)

        if last:
            for step in range(1, n_bal):
                source = lax.rem(me_b + n_bal - step, n_bal)
                pltpu.make_async_remote_copy(
                    src_ref=own_bal, dst_ref=bal_sums.at[source],
                    send_sem=bal_send.at[step], recv_sem=bal_recv.at[step],
                    device_id={"bal": source}, device_id_type=MESH,
                ).wait()
            summed = bal_sums[0]
            for index in range(1, n_bal):
                summed = summed + bal_sums[index]
            own_space[...] = summed
            space_sums[me_s] = summed
            for step in range(1, n_space):
                pltpu.make_async_remote_copy(
                    src_ref=own_space, dst_ref=space_sums.at[me_s],
                    send_sem=space_send.at[step], recv_sem=space_recv.at[step],
                    device_id={"space": lax.rem(me_s + step, n_space)}, device_id_type=MESH,
                ).start()
            solution_copy = pltpu.make_async_copy(solution_ref, solution_hbm, output_sem.at[0])
            solution_copy.start()
            for face in WAIT_ORDER:
                wait_face(turn, face)
                final = residual[:, span(face)] - (send[turn, face] + recv[turn, face])
                residual_ref[:, span(face)] = product(final, turned[face], CONTRACT_MIDDLE)
        else:
            rho_next = 1.0 / (2.0 * ratio_c - cheb_rho)
            running = None
            for face in WAIT_ORDER:
                wait_face(turn, face)
                updated = residual[:, span(face)] - (send[turn, face] + recv[turn, face])
                residual[:, span(face)] = updated
                moved = rho_next * cheb_rho * direction[:, span(face)] + 2.0 * rho_next / half_span * updated
                direction[:, span(face)] = moved
                total[:, span(face)] = total[:, span(face)] + moved
                running = project(face, running)
            cheb_rho = rho_next

    residual_copy = pltpu.make_async_copy(residual_ref, residual_hbm, output_sem.at[1])
    residual_copy.start()
    for step in range(1, n_space):
        source = lax.rem(me_s + n_space - step, n_space)
        pltpu.make_async_remote_copy(
            src_ref=own_space, dst_ref=space_sums.at[source],
            send_sem=space_send.at[step], recv_sem=space_recv.at[step],
            device_id={"space": source}, device_id_type=MESH,
        ).wait()
    summed = space_sums[0]
    for index in range(1, n_space):
        summed = summed + space_sums[index]
    violation_ref[...] = jnp.sqrt(summed[0:1, :loads] + 1e-06)
    violation_copy = pltpu.make_async_copy(violation_ref, violation_hbm, output_sem.at[2])
    violation_copy.start()

    for turn in range(ITERS + 1):
        for face in range(FACES):
            @pl.when(present[face])
            def _():
                face_copy(turn, face).wait_send()
    solution_copy.wait()
    residual_copy.wait()
    violation_copy.wait()


def finish(solution_in, residual_in, violation_in, solution_out, residual_out, violation_out, sems):
    pairs = ((solution_in, solution_out), (residual_in, residual_out), (violation_in, violation_out))
    copies = [
        pltpu.make_async_copy(source, target, sems.at[index]) for index, (source, target) in enumerate(pairs)
    ]
    for copy in copies:
        copy.start()
    for copy in copies:
        copy.wait()


def local(n_space, n_bal, panels, enrich, compliance, loads, face_maps, face_lengths, contact):
    rows, columns = panels.shape[2:]
    n_loads = loads.shape[2]
    face_len = columns // FACES
    width = -(-n_loads // 128) * 128
    hbm = pl.BlockSpec(memory_space=pltpu.HBM)
    turns = ITERS + 1
    flops = 2 * rows * columns * (face_len + ITERS * 4 * n_loads)
    field = (n_loads, columns)
    out = pl.pallas_call(
        functools.partial(kernel, n_space, n_bal),
        out_shape=(
            jax.ShapeDtypeStruct(field, jnp.float32),
            jax.ShapeDtypeStruct(field, jnp.float32),
            jax.ShapeDtypeStruct((1, n_loads), jnp.float32),
        ),
        in_specs=[hbm, pl.BlockSpec(memory_space=pltpu.SMEM)] + [hbm] * 5,
        out_specs=(hbm, hbm, hbm),
        scratch_shapes=[
            pltpu.SMEM((1, FACES), jnp.int32),
            pltpu.VMEM((FACES, face_len), jnp.int32),
            pltpu.VMEM((1, columns), jnp.float32),
            pltpu.VMEM((1, contact.shape[2]), jnp.int32),
            pltpu.VMEM(field, jnp.float32),
            pltpu.VMEM(field, jnp.float32),
            pltpu.VMEM(field, jnp.float32),
            pltpu.VMEM((1, n_loads), jnp.float32),
            pltpu.VMEM((FACES, face_len, face_len), jnp.bfloat16),
            pltpu.VMEM((rows, columns), jnp.bfloat16),
            pltpu.VMEM((rows, columns), jnp.bfloat16),
            pltpu.VMEM((rows, columns), jnp.bfloat16),
            pltpu.VMEM((FACES, face_len, face_len), jnp.bfloat16),
            pltpu.VMEM((16, columns), jnp.float32),
            pltpu.VMEM(field, jnp.float32),
            pltpu.VMEM(field, jnp.float32),
            pltpu.VMEM(field, jnp.float32),
            pltpu.VMEM((turns, FACES, n_loads, face_len), jnp.float32),
            pltpu.VMEM((turns, FACES, n_loads, face_len), jnp.float32),
            pltpu.VMEM((n_bal, 8, width), jnp.float32),
            pltpu.VMEM((n_space, 8, width), jnp.float32),
            pltpu.VMEM((8, width), jnp.float32),
            pltpu.VMEM((8, width), jnp.float32),
            pltpu.SemaphoreType.DMA((6,)),
            pltpu.SemaphoreType.DMA((3,)),
            pltpu.SemaphoreType.DMA((turns, FACES)),
            pltpu.SemaphoreType.DMA((turns, FACES)),
            pltpu.SemaphoreType.DMA((n_bal,)),
            pltpu.SemaphoreType.DMA((n_bal,)),
            pltpu.SemaphoreType.DMA((n_space,)),
            pltpu.SemaphoreType.DMA((n_space,)),
        ],
        compiler_params=pltpu.CompilerParams(
            collective_id=0, has_side_effects=True, vmem_limit_bytes=VMEM_BYTES
        ),
        cost_estimate=pl.CostEstimate(
            flops=flops, bytes_accessed=2 * rows * columns + 12 * n_loads * columns, transcendentals=n_loads
        ),
        name="feti",
    )(
        face_lengths[0], enrich, face_maps[0, 0], compliance[0], contact[0], loads[0, 0], panels[0, 0]
    )
    finished = pl.pallas_call(
        finish,
        out_shape=(
            jax.ShapeDtypeStruct(field, jnp.float32),
            jax.ShapeDtypeStruct(field, jnp.float32),
            jax.ShapeDtypeStruct((1, n_loads), jnp.float32),
        ),
        in_specs=[hbm] * 3,
        out_specs=(hbm, hbm, hbm),
        scratch_shapes=[pltpu.SemaphoreType.DMA((3,))],
        compiler_params=pltpu.CompilerParams(vmem_limit_bytes=VMEM_BYTES),
        name="finish",
    )(*out)
    return (finished[0][None, None], finished[1][None, None], finished[2][0])


def solution(mesh):
    in_specs = (
        P("space", "bal", None, None),
        P("space", "bal"),
        P("space", "bal", None),
        P("space", "bal", None, None),
        P("space", "bal", None, None),
        P("space", "bal", None),
        P("space", "bal", None),
    )
    out_specs = (P("space", "bal", None, None), P("space", "bal", None, None), P())
    body = functools.partial(local, mesh.shape["space"], mesh.shape["bal"])
    return jax.shard_map(body, mesh=mesh, in_specs=in_specs, out_specs=out_specs, check_vma=False)
```

```python
import functools
import math

import jax
import jax.numpy as jnp
from jax import lax
from jax.experimental import pallas as pl
from jax.experimental.pallas import tpu as pltpu
from jax.sharding import PartitionSpec as P

BLOCK_ROWS = 512
ITERS = 3
FACES = 4
HALVES = 2
VMEM_BYTES = 64 * 1024 * 1024
SEND_ORDER = (0, 1, 2, 3)
WAIT_ORDER = (2, 3, 0, 1)
MESH = pl.DeviceIdType.MESH
CONTRACT_LAST = (((1,), (1,)), ((), ()))
CONTRACT_MIDDLE = (((1,), (0,)), ((), ()))


def chebyshev_constants(iface, rows):
    upper = 2.6 * (1.0 + math.sqrt(iface / rows)) ** 2 + 4.0
    lower = 0.5
    center = (upper + lower) / 2.0
    half_span = (upper - lower) / 2.0
    return (center, half_span, center / half_span)


def parts(value, count):
    taken = []
    rest = value
    for index in range(count):
        part = rest.astype(jnp.bfloat16)
        taken.append(part)
        if index + 1 < count:
            rest = rest - part.astype(jnp.float32)
    return jnp.concatenate(taken, axis=0)


def product(value, matrix, dims, count=2):
    rows = value.shape[0]
    stacked = lax.dot_general(
        parts(value, count), matrix, dims, preferred_element_type=jnp.float32
    )
    total = stacked[:rows]
    for index in range(1, count):
        total = total + stacked[index * rows : (index + 1) * rows]
    return total


def kernel(
    n_space, n_bal,
    lengths_hbm, enrich_ref, maps_hbm, compliance_hbm, contact_hbm, loads_hbm, panel_hbm,
    solution_hbm, residual_hbm, violation_hbm,
    lengths_ref, maps_ref, compliance_ref, contact_ref, loads_ref,
    solution_ref, residual_ref, violation_ref, turned, panel, kept, kept_turned, onehot, diag, direction, total, residual, violated, send, recv, bal_sums, space_sums, own_bal, own_space,
    input_sem, output_sem, send_sem, recv_sem, bal_send, bal_recv, space_send, space_recv,
):
    me_s = lax.axis_index("space")
    me_b = lax.axis_index("bal")
    rows, columns = panel.shape
    face_len = columns // FACES
    loads = loads_ref.shape[0]
    center, half_span, ratio_c = chebyshev_constants(columns, rows)

    inputs = (
        (maps_hbm, maps_ref), (lengths_hbm, lengths_ref), (loads_hbm, loads_ref), (panel_hbm, panel),
        (compliance_hbm, compliance_ref), (contact_hbm, contact_ref),
    )
    copies = [
        pltpu.make_async_copy(source, target, input_sem.at[index])
        for index, (source, target) in enumerate(inputs)
    ]
    for copy in copies:
        copy.start()

    barrier = pltpu.get_barrier_semaphore()
    for step in range(1, n_bal):
        pl.semaphore_signal(
            barrier, inc=1, device_id={"bal": lax.rem(me_b + step, n_bal)}, device_id_type=MESH
        )
    for step in range(1, n_space):
        pl.semaphore_signal(
            barrier, inc=1, device_id={"space": lax.rem(me_s + step, n_space)}, device_id_type=MESH
        )

    present = (me_s > 0, me_s < n_space - 1, me_b > 0, me_b < n_bal - 1)
    across = (
        {"space": jnp.maximum(me_s - 1, 0)},
        {"space": jnp.minimum(me_s + 1, n_space - 1)},
        {"bal": jnp.maximum(me_b - 1, 0)},
        {"bal": jnp.minimum(me_b + 1, n_bal - 1)},
    )
    part = loads // HALVES

    def face_copy(turn, half, face):
        return pltpu.make_async_remote_copy(
            src_ref=send.at[turn, half, face],
            dst_ref=recv.at[turn, half, face ^ 1],
            send_sem=send_sem.at[turn, half, face],
            recv_sem=recv_sem.at[turn, half, face ^ 1],
            device_id=across[face],
            device_id_type=MESH,
        )

    def start_face(turn, half, face):
        @pl.when(present[face])
        def _():
            face_copy(turn, half, face).start()

    def wait_face(turn, half, face):
        @pl.when(present[face])
        def _():
            face_copy(turn, half, face ^ 1).wait_recv()

    def lines(half):
        return slice(half * part, (half + 1) * part)

    def span(face):
        return slice(face * face_len, (face + 1) * face_len)

    copies[0].wait()
    copies[1].wait()
    row_of = lax.broadcasted_iota(jnp.int32, (face_len, face_len), 0)
    slot_of = lax.broadcasted_iota(jnp.int32, (face_len, face_len), 1)
    for face in range(FACES):
        table = jnp.broadcast_to(maps_ref[face : face + 1, :], (face_len, face_len))
        hit = (row_of == table) & (slot_of < lengths_ref[0, face])
        onehot[face] = jnp.where(hit, 1.0, 0.0).astype(jnp.bfloat16)

    copies[2].wait()
    for face in SEND_ORDER:
        canonical = product(loads_ref[:, span(face)], onehot[face], CONTRACT_MIDDLE)
        for half in range(HALVES):
            send[0, half, face] = canonical[lines(half)]

    pl.semaphore_wait(barrier, n_bal - 1 + n_space - 1)
    for half in range(HALVES):
        for face in SEND_ORDER:
            start_face(0, half, face)

    for face in range(FACES):
        @pl.when(jnp.logical_not(present[face]))
        def _():
            for turn in range(ITERS + 1):
                for half in range(HALVES):
                    recv[turn, half, face] = jnp.zeros((part, face_len), jnp.float32)

    for index in range(4, len(copies)):
        copies[index].wait()
    for face in range(FACES):
        turned[face] = onehot[face].T
        wide = jnp.broadcast_to(compliance_ref[:, span(face)], (16, face_len))
        diag[:, span(face)] = product(wide, onehot[face], CONTRACT_MIDDLE, 3)

    lane = 128
    contact = contact_ref[...]
    groups = columns // lane
    group_rows = max(groups, 8)
    group_of = lax.broadcasted_iota(jnp.int32, (group_rows, contact.shape[1]), 0)
    place_of = lax.broadcasted_iota(jnp.int32, (lane, contact.shape[1]), 0)
    in_group = jnp.where(group_of == lax.shift_right_logical(contact, 7), 1.0, 0.0)
    at_place = jnp.where(place_of == (contact & (lane - 1)), 1.0, 0.0)
    counts = lax.dot_general(
        in_group.astype(jnp.bfloat16), at_place.astype(jnp.bfloat16), CONTRACT_LAST,
        preferred_element_type=jnp.float32,
    )

    copies[3].wait()
    live_rows = enrich_ref[0, 0] * BLOCK_ROWS
    keep = lax.broadcasted_iota(jnp.int32, (rows, face_len), 0) < live_rows
    for face in range(FACES):
        picked = jnp.dot(panel[:, span(face)], onehot[face], preferred_element_type=jnp.float32)
        masked = jnp.where(keep, picked, 0.0).astype(jnp.bfloat16)
        kept[:, span(face)] = masked
        kept_turned[span(face), :] = masked.T

    def project(half, face, running):
        term = jnp.dot(
            parts(direction[lines(half), span(face)], 2), kept_turned[span(face), :],
            preferred_element_type=jnp.float32,
        )
        return term if running is None else running + term

    def apply(turn, half, running):
        projected = parts(running[:part] + running[part:], 2)
        for face in SEND_ORDER:
            stacked = jnp.dot(projected, kept[:, span(face)], preferred_element_type=jnp.float32)
            send[turn, half, face] = (
                stacked[:part] + stacked[part:] + direction[lines(half), span(face)] * diag[0:1, span(face)]
            )
            start_face(turn, half, face)

    for half in range(HALVES):
        running = None
        for face in WAIT_ORDER:
            wait_face(0, half, face)
            first = send[0, half, face] + recv[0, half, face]
            residual[lines(half), span(face)] = first
            direction[lines(half), span(face)] = first / center
            total[lines(half), span(face)] = first / center
            running = project(half, face, running)
        apply(1, half, running)

    def weigh(half):
        weighted = jnp.zeros((part, lane), jnp.float32)
        for face in range(FACES):
            local = product(total[lines(half), span(face)], turned[face], CONTRACT_MIDDLE)
            solution_ref[lines(half), span(face)] = local
            negative = jnp.minimum(local, 0.0)
            squares = negative * negative
            for piece in range(face_len // lane):
                group = face * (face_len // lane) + piece
                weighted = weighted + squares[:, piece * lane : (piece + 1) * lane] * counts[group : group + 1, :]
        violated[lines(half), :] = weighted

    cheb_rho = 1.0 / ratio_c
    for turn in range(1, ITERS):
        rho_next = 1.0 / (2.0 * ratio_c - cheb_rho)
        for half in range(HALVES):
            running = None
            for face in WAIT_ORDER:
                wait_face(turn, half, face)
                updated = residual[lines(half), span(face)] - (send[turn, half, face] + recv[turn, half, face])
                residual[lines(half), span(face)] = updated
                moved = (
                    rho_next * cheb_rho * direction[lines(half), span(face)] + 2.0 * rho_next / half_span * updated
                )
                direction[lines(half), span(face)] = moved
                total[lines(half), span(face)] = total[lines(half), span(face)] + moved
                running = project(half, face, running)
            apply(turn + 1, half, running)
            if turn + 1 == ITERS:
                weigh(half)
        cheb_rho = rho_next

    pieces = parts(violated[...], 3)
    ones = jnp.ones((16, lane), jnp.bfloat16)
    spread = lax.dot_general(ones, pieces, CONTRACT_LAST, preferred_element_type=jnp.float32)
    terms = spread[:8, :loads] + spread[:8, loads : 2 * loads] + spread[:8, 2 * loads :]
    own_bal[:, loads:] = jnp.zeros((8, own_bal.shape[1] - loads), jnp.float32)
    own_bal[:, :loads] = terms
    bal_sums[me_b] = own_bal[...]
    for step in range(1, n_bal):
        pltpu.make_async_remote_copy(
            src_ref=own_bal, dst_ref=bal_sums.at[me_b],
            send_sem=bal_send.at[step], recv_sem=bal_recv.at[step],
            device_id={"bal": lax.rem(me_b + step, n_bal)}, device_id_type=MESH,
        ).start()
    solution_copy = pltpu.make_async_copy(solution_ref, solution_hbm, output_sem.at[0])
    solution_copy.start()

    def settle(half):
        for face in WAIT_ORDER:
            wait_face(ITERS, half, face)
            final = residual[lines(half), span(face)] - (send[ITERS, half, face] + recv[ITERS, half, face])
            residual_ref[lines(half), span(face)] = product(final, turned[face], CONTRACT_MIDDLE)
        copy = pltpu.make_async_copy(
            residual_ref.at[lines(half)], residual_hbm.at[lines(half)], output_sem.at[2 + half]
        )
        copy.start()
        return copy

    residual_copies = [settle(0)]

    for step in range(1, n_bal):
        source = lax.rem(me_b + n_bal - step, n_bal)
        pltpu.make_async_remote_copy(
            src_ref=own_bal, dst_ref=bal_sums.at[source],
            send_sem=bal_send.at[step], recv_sem=bal_recv.at[step],
            device_id={"bal": source}, device_id_type=MESH,
        ).wait()
    summed = bal_sums[0]
    for index in range(1, n_bal):
        summed = summed + bal_sums[index]
    own_space[...] = summed
    space_sums[me_s] = summed
    for step in range(1, n_space):
        pltpu.make_async_remote_copy(
            src_ref=own_space, dst_ref=space_sums.at[me_s],
            send_sem=space_send.at[step], recv_sem=space_recv.at[step],
            device_id={"space": lax.rem(me_s + step, n_space)}, device_id_type=MESH,
        ).start()

    for half in range(1, HALVES):
        residual_copies.append(settle(half))

    for step in range(1, n_space):
        source = lax.rem(me_s + n_space - step, n_space)
        pltpu.make_async_remote_copy(
            src_ref=own_space, dst_ref=space_sums.at[source],
            send_sem=space_send.at[step], recv_sem=space_recv.at[step],
            device_id={"space": source}, device_id_type=MESH,
        ).wait()
    summed = space_sums[0]
    for index in range(1, n_space):
        summed = summed + space_sums[index]
    violation_ref[...] = jnp.sqrt(summed[0:1, :loads] + 1e-06)
    violation_copy = pltpu.make_async_copy(violation_ref, violation_hbm, output_sem.at[1])
    violation_copy.start()

    for turn in range(ITERS + 1):
        for face in range(FACES):
            @pl.when(present[face])
            def _():
                for half in range(HALVES):
                    face_copy(turn, half, face).wait_send()
    solution_copy.wait()
    violation_copy.wait()
    for copy in residual_copies:
        copy.wait()


def finish(
    solution_in, residual_in, violation_in, solution_out, residual_out, violation_out,
    solution_held, residual_held, violation_held, in_sems, out_sems,
):
    rows = solution_held.shape[0]
    part = rows // HALVES
    moves = [(violation_in, violation_held, violation_out)]
    for half in range(HALVES):
        span = slice(half * part, (half + 1) * part)
        moves.append((residual_in.at[span], residual_held.at[span], residual_out.at[span]))
        moves.append((solution_in.at[span], solution_held.at[span], solution_out.at[span]))
    fetches = [
        pltpu.make_async_copy(source, held, in_sems.at[index]) for index, (source, held, _) in enumerate(moves)
    ]
    stores = [
        pltpu.make_async_copy(held, target, out_sems.at[index]) for index, (_, held, target) in enumerate(moves)
    ]
    for fetch in fetches:
        fetch.start()
    for fetch, store in zip(fetches, stores):
        fetch.wait()
        store.start()
    for store in stores:
        store.wait()


def local(n_space, n_bal, panels, enrich, compliance, loads, face_maps, face_lengths, contact):
    rows, columns = panels.shape[2:]
    n_loads = loads.shape[2]
    face_len = columns // FACES
    width = -(-n_loads // 128) * 128
    hbm = pl.BlockSpec(memory_space=pltpu.HBM)
    turns = ITERS + 1
    flops = 2 * rows * columns * (face_len + ITERS * 4 * n_loads)
    field = (n_loads, columns)
    out = pl.pallas_call(
        functools.partial(kernel, n_space, n_bal),
        out_shape=(
            jax.ShapeDtypeStruct(field, jnp.float32),
            jax.ShapeDtypeStruct(field, jnp.float32),
            jax.ShapeDtypeStruct((1, n_loads), jnp.float32),
        ),
        in_specs=[hbm, pl.BlockSpec(memory_space=pltpu.SMEM)] + [hbm] * 5,
        out_specs=(hbm, hbm, hbm),
        scratch_shapes=[
            pltpu.SMEM((1, FACES), jnp.int32),
            pltpu.VMEM((FACES, face_len), jnp.int32),
            pltpu.VMEM((1, columns), jnp.float32),
            pltpu.VMEM((1, contact.shape[2]), jnp.int32),
            pltpu.VMEM(field, jnp.float32),
            pltpu.VMEM(field, jnp.float32),
            pltpu.VMEM(field, jnp.float32),
            pltpu.VMEM((1, n_loads), jnp.float32),
            pltpu.VMEM((FACES, face_len, face_len), jnp.bfloat16),
            pltpu.VMEM((rows, columns), jnp.bfloat16),
            pltpu.VMEM((rows, columns), jnp.bfloat16),
            pltpu.VMEM((rows, columns), jnp.bfloat16),
            pltpu.VMEM((FACES, face_len, face_len), jnp.bfloat16),
            pltpu.VMEM((16, columns), jnp.float32),
            pltpu.VMEM(field, jnp.float32),
            pltpu.VMEM(field, jnp.float32),
            pltpu.VMEM(field, jnp.float32),
            pltpu.VMEM((n_loads, 128), jnp.float32),
            pltpu.VMEM((turns, HALVES, FACES, n_loads // HALVES, face_len), jnp.float32),
            pltpu.VMEM((turns, HALVES, FACES, n_loads // HALVES, face_len), jnp.float32),
            pltpu.VMEM((n_bal, 8, width), jnp.float32),
            pltpu.VMEM((n_space, 8, width), jnp.float32),
            pltpu.VMEM((8, width), jnp.float32),
            pltpu.VMEM((8, width), jnp.float32),
            pltpu.SemaphoreType.DMA((6,)),
            pltpu.SemaphoreType.DMA((2 + HALVES,)),
            pltpu.SemaphoreType.DMA((turns, HALVES, FACES)),
            pltpu.SemaphoreType.DMA((turns, HALVES, FACES)),
            pltpu.SemaphoreType.DMA((n_bal,)),
            pltpu.SemaphoreType.DMA((n_bal,)),
            pltpu.SemaphoreType.DMA((n_space,)),
            pltpu.SemaphoreType.DMA((n_space,)),
        ],
        compiler_params=pltpu.CompilerParams(
            collective_id=0, has_side_effects=True, vmem_limit_bytes=VMEM_BYTES
        ),
        cost_estimate=pl.CostEstimate(
            flops=flops, bytes_accessed=2 * rows * columns + 12 * n_loads * columns, transcendentals=n_loads
        ),
        name="feti",
    )(
        face_lengths[0], enrich, face_maps[0, 0], compliance[0], contact[0], loads[0, 0], panels[0, 0]
    )
    finished = pl.pallas_call(
        finish,
        out_shape=(
            jax.ShapeDtypeStruct(field, jnp.float32),
            jax.ShapeDtypeStruct(field, jnp.float32),
            jax.ShapeDtypeStruct((1, n_loads), jnp.float32),
        ),
        in_specs=[hbm] * 3,
        out_specs=(hbm, hbm, hbm),
        scratch_shapes=[
            pltpu.VMEM(field, jnp.float32),
            pltpu.VMEM(field, jnp.float32),
            pltpu.VMEM((1, n_loads), jnp.float32),
            pltpu.SemaphoreType.DMA((1 + 2 * HALVES,)),
            pltpu.SemaphoreType.DMA((1 + 2 * HALVES,)),
        ],
        compiler_params=pltpu.CompilerParams(vmem_limit_bytes=VMEM_BYTES),
        name="finish",
    )(*out)
    return (finished[0][None, None], finished[1][None, None], finished[2][0])


def solution(mesh):
    in_specs = (
        P("space", "bal", None, None),
        P("space", "bal"),
        P("space", "bal", None),
        P("space", "bal", None, None),
        P("space", "bal", None, None),
        P("space", "bal", None),
        P("space", "bal", None),
    )
    out_specs = (P("space", "bal", None, None), P("space", "bal", None, None), P())
    body = functools.partial(local, mesh.shape["space"], mesh.shape["bal"])
    return jax.shard_map(body, mesh=mesh, in_specs=in_specs, out_specs=out_specs, check_vma=False)
```

```python
import functools
import math

import jax
import jax.numpy as jnp
from jax import lax
from jax.experimental import pallas as pl
from jax.experimental.pallas import tpu as pltpu
from jax.sharding import PartitionSpec as P

BLOCK_ROWS = 512
ITERS = 3
FACES = 4
HALVES = 1
VMEM_BYTES = 64 * 1024 * 1024
SPACE_PAIR = (0, 1)
BAL_PAIR = (2, 3)
MESH = pl.DeviceIdType.MESH
CONTRACT_LAST = (((1,), (1,)), ((), ()))
CONTRACT_MIDDLE = (((1,), (0,)), ((), ()))


def chebyshev_constants(iface, rows):
    upper = 2.6 * (1.0 + math.sqrt(iface / rows)) ** 2 + 4.0
    lower = 0.5
    center = (upper + lower) / 2.0
    half_span = (upper - lower) / 2.0
    return (center, half_span, center / half_span)


def parts(value, count):
    taken = []
    rest = value
    for index in range(count):
        part = rest.astype(jnp.bfloat16)
        taken.append(part)
        if index + 1 < count:
            rest = rest - part.astype(jnp.float32)
    return jnp.concatenate(taken, axis=0)


def product(value, matrix, dims, count=2):
    rows = value.shape[0]
    stacked = lax.dot_general(
        parts(value, count), matrix, dims, preferred_element_type=jnp.float32
    )
    total = stacked[:rows]
    for index in range(1, count):
        total = total + stacked[index * rows : (index + 1) * rows]
    return total


def kernel(
    n_space, n_bal,
    lengths_hbm, enrich_ref, maps_hbm, compliance_hbm, contact_hbm, loads_hbm, panel_hbm,
    solution_hbm, residual_hbm, violation_hbm,
    lengths_ref, maps_ref, compliance_ref, contact_ref, loads_ref,
    solution_ref, residual_ref, violation_ref, turned, panel, kept, kept_turned, onehot, diag, weights, direction, total, residual, violated, send, recv, bal_sums, space_sums, own_bal, own_space,
    input_sem, output_sem, send_sem, recv_sem, bal_send, bal_recv, space_send, space_recv,
):
    me_s = lax.axis_index("space")
    me_b = lax.axis_index("bal")
    rows, columns = panel.shape
    face_len = columns // FACES
    loads = loads_ref.shape[0]
    center, half_span, ratio_c = chebyshev_constants(columns, rows)

    inputs = (
        (maps_hbm, maps_ref), (lengths_hbm, lengths_ref), (loads_hbm, loads_ref), (panel_hbm, panel),
        (compliance_hbm, compliance_ref), (contact_hbm, contact_ref),
    )
    copies = [
        pltpu.make_async_copy(source, target, input_sem.at[index])
        for index, (source, target) in enumerate(inputs)
    ]
    for copy in copies:
        copy.start()

    barrier = pltpu.get_barrier_semaphore()
    for step in range(1, n_bal):
        pl.semaphore_signal(
            barrier, inc=1, device_id={"bal": lax.rem(me_b + step, n_bal)}, device_id_type=MESH
        )
    for step in range(1, n_space):
        pl.semaphore_signal(
            barrier, inc=1, device_id={"space": lax.rem(me_s + step, n_space)}, device_id_type=MESH
        )

    present = (me_s > 0, me_s < n_space - 1, me_b > 0, me_b < n_bal - 1)
    across = (
        {"space": jnp.maximum(me_s - 1, 0)},
        {"space": jnp.minimum(me_s + 1, n_space - 1)},
        {"bal": jnp.maximum(me_b - 1, 0)},
        {"bal": jnp.minimum(me_b + 1, n_bal - 1)},
    )
    part = loads // HALVES

    def face_copy(turn, half, face):
        return pltpu.make_async_remote_copy(
            src_ref=send.at[turn, half, face],
            dst_ref=recv.at[turn, half, face ^ 1],
            send_sem=send_sem.at[turn, half, face],
            recv_sem=recv_sem.at[turn, half, face ^ 1],
            device_id=across[face],
            device_id_type=MESH,
        )

    def start_face(turn, half, face):
        @pl.when(present[face])
        def _():
            face_copy(turn, half, face).start()

    def wait_face(turn, half, face):
        @pl.when(present[face])
        def _():
            face_copy(turn, half, face ^ 1).wait_recv()

    def lines(half):
        return slice(half * part, (half + 1) * part)

    def span(face):
        return slice(face * face_len, (face + 1) * face_len)

    copies[0].wait()
    copies[1].wait()
    row_of = lax.broadcasted_iota(jnp.int32, (face_len, face_len), 0)
    slot_of = lax.broadcasted_iota(jnp.int32, (face_len, face_len), 1)
    for face in range(FACES):
        table = jnp.broadcast_to(maps_ref[face : face + 1, :], (face_len, face_len))
        hit = (row_of == table) & (slot_of < lengths_ref[0, face])
        onehot[face] = jnp.where(hit, 1.0, 0.0).astype(jnp.bfloat16)

    copies[2].wait()
    for face in SPACE_PAIR + BAL_PAIR:
        canonical = product(loads_ref[:, span(face)], onehot[face], CONTRACT_MIDDLE)
        for half in range(HALVES):
            send[0, half, face] = canonical[lines(half)]

    pl.semaphore_wait(barrier, n_bal - 1 + n_space - 1)
    for half in range(HALVES):
        for face in SPACE_PAIR + BAL_PAIR:
            start_face(0, half, face)

    for face in range(FACES):
        @pl.when(jnp.logical_not(present[face]))
        def _():
            for turn in range(ITERS + 1):
                for half in range(HALVES):
                    recv[turn, half, face] = jnp.zeros((part, face_len), jnp.float32)

    for index in range(4, len(copies)):
        copies[index].wait()
    for face in range(FACES):
        turned[face] = onehot[face].T
        wide = jnp.broadcast_to(compliance_ref[:, span(face)], (16, face_len))
        diag[:, span(face)] = product(wide, onehot[face], CONTRACT_MIDDLE, 3)

    lane = 128
    contact = contact_ref[...]
    groups = columns // lane
    group_rows = max(groups, 8)
    group_of = lax.broadcasted_iota(jnp.int32, (group_rows, contact.shape[1]), 0)
    place_of = lax.broadcasted_iota(jnp.int32, (lane, contact.shape[1]), 0)
    in_group = jnp.where(group_of == lax.shift_right_logical(contact, 7), 1.0, 0.0)
    at_place = jnp.where(place_of == (contact & (lane - 1)), 1.0, 0.0)
    counts = lax.dot_general(
        in_group.astype(jnp.bfloat16), at_place.astype(jnp.bfloat16), CONTRACT_LAST,
        preferred_element_type=jnp.float32,
    )

    per_face = face_len // lane
    for face in range(FACES):
        weight = jnp.zeros((16, face_len), jnp.float32)
        for piece in range(per_face):
            group = face * per_face + piece
            row = jnp.broadcast_to(counts[group : group + 1, :], (16, lane)).astype(jnp.bfloat16)
            weight = weight + jnp.dot(
                row, onehot[face, piece * lane : (piece + 1) * lane, :], preferred_element_type=jnp.float32
            )
        weights[:, span(face)] = weight

    copies[3].wait()
    live_rows = enrich_ref[0, 0] * BLOCK_ROWS
    keep = lax.broadcasted_iota(jnp.int32, (rows, face_len), 0) < live_rows
    for face in range(FACES):
        picked = jnp.dot(panel[:, span(face)], onehot[face], preferred_element_type=jnp.float32)
        masked = jnp.where(keep, picked, 0.0).astype(jnp.bfloat16)
        kept[:, span(face)] = masked
        kept_turned[span(face), :] = masked.T

    def pair_span(pair):
        return slice(pair[0] * face_len, (pair[-1] + 1) * face_len)

    def project(half, pair, running):
        term = jnp.dot(
            parts(direction[lines(half), pair_span(pair)], 2), kept_turned[pair_span(pair), :],
            preferred_element_type=jnp.float32,
        )
        return term if running is None else running + term

    def apply(turn, half, running):
        projected = parts(running[:part] + running[part:], 2)
        for pair in (SPACE_PAIR, BAL_PAIR):
            stacked = jnp.dot(projected, kept[:, pair_span(pair)], preferred_element_type=jnp.float32)
            image = (
                stacked[:part] + stacked[part:]
                + direction[lines(half), pair_span(pair)] * diag[0:1, pair_span(pair)]
            )
            for index, face in enumerate(pair):
                send[turn, half, face] = image[:, index * face_len : (index + 1) * face_len]
            for face in pair:
                start_face(turn, half, face)

    def share_violation():
        pieces = parts(violated[...], 3)
        ones = jnp.ones((16, lane), jnp.bfloat16)
        spread = lax.dot_general(ones, pieces, CONTRACT_LAST, preferred_element_type=jnp.float32)
        terms = spread[:8, :loads] + spread[:8, loads : 2 * loads] + spread[:8, 2 * loads :]
        own_bal[:, loads:] = jnp.zeros((8, own_bal.shape[1] - loads), jnp.float32)
        own_bal[:, :loads] = terms
        bal_sums[me_b] = own_bal[...]
        for step in range(1, n_bal):
            pltpu.make_async_remote_copy(
                src_ref=own_bal, dst_ref=bal_sums.at[me_b],
                send_sem=bal_send.at[step], recv_sem=bal_recv.at[step],
                device_id={"bal": lax.rem(me_b + step, n_bal)}, device_id_type=MESH,
            ).start()

    for half in range(HALVES):
        running = None
        for pair in (BAL_PAIR, SPACE_PAIR):
            for face in pair:
                wait_face(0, half, face)
            for face in pair:
                first = send[0, half, face] + recv[0, half, face]
                residual[lines(half), span(face)] = first
                direction[lines(half), span(face)] = first * (1.0 / center)
                total[lines(half), span(face)] = first * (1.0 / center)
            running = project(half, pair, running)
        apply(1, half, running)

    cheb_rho = 1.0 / ratio_c
    for turn in range(1, ITERS):
        rho_next = 1.0 / (2.0 * ratio_c - cheb_rho)
        for half in range(HALVES):
            running = None
            weighted = jnp.zeros((part, face_len), jnp.float32)
            for pair in (BAL_PAIR, SPACE_PAIR):
                for face in pair:
                    wait_face(turn, half, face)
                for face in pair:
                    updated = residual[lines(half), span(face)] - (send[turn, half, face] + recv[turn, half, face])
                    residual[lines(half), span(face)] = updated
                    moved = (
                        rho_next * cheb_rho * direction[lines(half), span(face)]
                        + 2.0 * rho_next / half_span * updated
                    )
                    direction[lines(half), span(face)] = moved
                    summed = total[lines(half), span(face)] + moved
                    total[lines(half), span(face)] = summed
                    negative = jnp.minimum(summed, 0.0)
                    weighted = weighted + negative * negative * weights[0:1, span(face)]
                running = project(half, pair, running)
            if turn + 1 == ITERS:
                narrow = weighted[:, :lane]
                for piece in range(1, per_face):
                    narrow = narrow + weighted[:, piece * lane : (piece + 1) * lane]
                violated[lines(half), :] = narrow
                if half + 1 == HALVES:
                    share_violation()
            apply(turn + 1, half, running)
        cheb_rho = rho_next

    for face in range(FACES):
        solution_ref[:, span(face)] = product(total[:, span(face)], turned[face], CONTRACT_MIDDLE)
    solution_copy = pltpu.make_async_copy(solution_ref, solution_hbm, output_sem.at[0])
    solution_copy.start()

    def settle(half):
        for pair in (BAL_PAIR, SPACE_PAIR):
            for face in pair:
                wait_face(ITERS, half, face)
            for face in pair:
                final = residual[lines(half), span(face)] - (send[ITERS, half, face] + recv[ITERS, half, face])
                residual_ref[lines(half), span(face)] = product(final, turned[face], CONTRACT_MIDDLE)
        copy = pltpu.make_async_copy(
            residual_ref.at[lines(half)], residual_hbm.at[lines(half)], output_sem.at[2 + half]
        )
        copy.start()
        return copy


    for step in range(1, n_bal):
        source = lax.rem(me_b + n_bal - step, n_bal)
        pltpu.make_async_remote_copy(
            src_ref=own_bal, dst_ref=bal_sums.at[source],
            send_sem=bal_send.at[step], recv_sem=bal_recv.at[step],
            device_id={"bal": source}, device_id_type=MESH,
        ).wait()
    summed = bal_sums[0]
    for index in range(1, n_bal):
        summed = summed + bal_sums[index]
    own_space[...] = summed
    space_sums[me_s] = summed
    for step in range(1, n_space):
        pltpu.make_async_remote_copy(
            src_ref=own_space, dst_ref=space_sums.at[me_s],
            send_sem=space_send.at[step], recv_sem=space_recv.at[step],
            device_id={"space": lax.rem(me_s + step, n_space)}, device_id_type=MESH,
        ).start()

    residual_copies = [settle(half) for half in range(HALVES)]

    for step in range(1, n_space):
        source = lax.rem(me_s + n_space - step, n_space)
        pltpu.make_async_remote_copy(
            src_ref=own_space, dst_ref=space_sums.at[source],
            send_sem=space_send.at[step], recv_sem=space_recv.at[step],
            device_id={"space": source}, device_id_type=MESH,
        ).wait()
    summed = space_sums[0]
    for index in range(1, n_space):
        summed = summed + space_sums[index]
    violation_ref[...] = jnp.sqrt(summed[0:1, :loads] + 1e-06)
    violation_copy = pltpu.make_async_copy(violation_ref, violation_hbm, output_sem.at[1])
    violation_copy.start()

    for turn in range(ITERS + 1):
        for face in range(FACES):
            @pl.when(present[face])
            def _():
                for half in range(HALVES):
                    face_copy(turn, half, face).wait_send()
    solution_copy.wait()
    violation_copy.wait()
    for copy in residual_copies:
        copy.wait()


def finish(
    solution_in, residual_in, violation_in, solution_out, residual_out, violation_out,
    solution_held, residual_held, violation_held, in_sems, out_sems,
):
    rows = solution_held.shape[0]
    part = rows // HALVES
    moves = [(violation_in, violation_held, violation_out)]
    for half in range(HALVES):
        span = slice(half * part, (half + 1) * part)
        moves.append((residual_in.at[span], residual_held.at[span], residual_out.at[span]))
        moves.append((solution_in.at[span], solution_held.at[span], solution_out.at[span]))
    fetches = [
        pltpu.make_async_copy(source, held, in_sems.at[index]) for index, (source, held, _) in enumerate(moves)
    ]
    stores = [
        pltpu.make_async_copy(held, target, out_sems.at[index]) for index, (_, held, target) in enumerate(moves)
    ]
    for fetch in fetches:
        fetch.start()
    for fetch, store in zip(fetches, stores):
        fetch.wait()
        store.start()
    for store in stores:
        store.wait()


def local(n_space, n_bal, panels, enrich, compliance, loads, face_maps, face_lengths, contact):
    rows, columns = panels.shape[2:]
    n_loads = loads.shape[2]
    face_len = columns // FACES
    width = -(-n_loads // 128) * 128
    hbm = pl.BlockSpec(memory_space=pltpu.HBM)
    turns = ITERS + 1
    flops = 2 * rows * columns * (face_len + ITERS * 4 * n_loads)
    field = (n_loads, columns)
    out = pl.pallas_call(
        functools.partial(kernel, n_space, n_bal),
        out_shape=(
            jax.ShapeDtypeStruct(field, jnp.float32),
            jax.ShapeDtypeStruct(field, jnp.float32),
            jax.ShapeDtypeStruct((1, n_loads), jnp.float32),
        ),
        in_specs=[hbm, pl.BlockSpec(memory_space=pltpu.SMEM)] + [hbm] * 5,
        out_specs=(hbm, hbm, hbm),
        scratch_shapes=[
            pltpu.SMEM((1, FACES), jnp.int32),
            pltpu.VMEM((FACES, face_len), jnp.int32),
            pltpu.VMEM((1, columns), jnp.float32),
            pltpu.VMEM((1, contact.shape[2]), jnp.int32),
            pltpu.VMEM(field, jnp.float32),
            pltpu.VMEM(field, jnp.float32),
            pltpu.VMEM(field, jnp.float32),
            pltpu.VMEM((1, n_loads), jnp.float32),
            pltpu.VMEM((FACES, face_len, face_len), jnp.bfloat16),
            pltpu.VMEM((rows, columns), jnp.bfloat16),
            pltpu.VMEM((rows, columns), jnp.bfloat16),
            pltpu.VMEM((rows, columns), jnp.bfloat16),
            pltpu.VMEM((FACES, face_len, face_len), jnp.bfloat16),
            pltpu.VMEM((16, columns), jnp.float32),
            pltpu.VMEM((16, columns), jnp.float32),
            pltpu.VMEM(field, jnp.float32),
            pltpu.VMEM(field, jnp.float32),
            pltpu.VMEM(field, jnp.float32),
            pltpu.VMEM((n_loads, 128), jnp.float32),
            pltpu.VMEM((turns, HALVES, FACES, n_loads // HALVES, face_len), jnp.float32),
            pltpu.VMEM((turns, HALVES, FACES, n_loads // HALVES, face_len), jnp.float32),
            pltpu.VMEM((n_bal, 8, width), jnp.float32),
            pltpu.VMEM((n_space, 8, width), jnp.float32),
            pltpu.VMEM((8, width), jnp.float32),
            pltpu.VMEM((8, width), jnp.float32),
            pltpu.SemaphoreType.DMA((6,)),
            pltpu.SemaphoreType.DMA((2 + HALVES,)),
            pltpu.SemaphoreType.DMA((turns, HALVES, FACES)),
            pltpu.SemaphoreType.DMA((turns, HALVES, FACES)),
            pltpu.SemaphoreType.DMA((n_bal,)),
            pltpu.SemaphoreType.DMA((n_bal,)),
            pltpu.SemaphoreType.DMA((n_space,)),
            pltpu.SemaphoreType.DMA((n_space,)),
        ],
        compiler_params=pltpu.CompilerParams(
            collective_id=0, has_side_effects=True, vmem_limit_bytes=VMEM_BYTES
        ),
        cost_estimate=pl.CostEstimate(
            flops=flops, bytes_accessed=2 * rows * columns + 12 * n_loads * columns, transcendentals=n_loads
        ),
        name="feti",
    )(
        face_lengths[0], enrich, face_maps[0, 0], compliance[0], contact[0], loads[0, 0], panels[0, 0]
    )
    finished = pl.pallas_call(
        finish,
        out_shape=(
            jax.ShapeDtypeStruct(field, jnp.float32),
            jax.ShapeDtypeStruct(field, jnp.float32),
            jax.ShapeDtypeStruct((1, n_loads), jnp.float32),
        ),
        in_specs=[hbm] * 3,
        out_specs=(hbm, hbm, hbm),
        scratch_shapes=[
            pltpu.VMEM(field, jnp.float32),
            pltpu.VMEM(field, jnp.float32),
            pltpu.VMEM((1, n_loads), jnp.float32),
            pltpu.SemaphoreType.DMA((1 + 2 * HALVES,)),
            pltpu.SemaphoreType.DMA((1 + 2 * HALVES,)),
        ],
        compiler_params=pltpu.CompilerParams(vmem_limit_bytes=VMEM_BYTES),
        name="finish",
    )(*out)
    return (finished[0][None, None], finished[1][None, None], finished[2][0])


def solution(mesh):
    in_specs = (
        P("space", "bal", None, None),
        P("space", "bal"),
        P("space", "bal", None),
        P("space", "bal", None, None),
        P("space", "bal", None, None),
        P("space", "bal", None),
        P("space", "bal", None),
    )
    out_specs = (P("space", "bal", None, None), P("space", "bal", None, None), P())
    body = functools.partial(local, mesh.shape["space"], mesh.shape["bal"])
    return jax.shard_map(body, mesh=mesh, in_specs=in_specs, out_specs=out_specs, check_vma=False)
```

```python
import functools
import math

import jax
import jax.numpy as jnp
from jax import lax
from jax.experimental import pallas as pl
from jax.experimental.pallas import tpu as pltpu
from jax.sharding import PartitionSpec as P

BLOCK_ROWS = 512
ITERS = 3
FACES = 4
HALVES = 1
VMEM_BYTES = 64 * 1024 * 1024
SPACE_PAIR = (0, 1)
BAL_PAIR = (2, 3)
MESH = pl.DeviceIdType.MESH
CONTRACT_LAST = (((1,), (1,)), ((), ()))
CONTRACT_MIDDLE = (((1,), (0,)), ((), ()))


def chebyshev_constants(iface, rows):
    upper = 2.6 * (1.0 + math.sqrt(iface / rows)) ** 2 + 4.0
    lower = 0.5
    center = (upper + lower) / 2.0
    half_span = (upper - lower) / 2.0
    return (center, half_span, center / half_span)


def parts(value, count):
    taken = []
    rest = value
    for index in range(count):
        part = rest.astype(jnp.bfloat16)
        taken.append(part)
        if index + 1 < count:
            rest = rest - part.astype(jnp.float32)
    return jnp.concatenate(taken, axis=0)


def product(value, matrix, dims, count=2):
    rows = value.shape[0]
    stacked = lax.dot_general(
        parts(value, count), matrix, dims, preferred_element_type=jnp.float32
    )
    total = stacked[:rows]
    for index in range(1, count):
        total = total + stacked[index * rows : (index + 1) * rows]
    return total


def kernel(
    n_space, n_bal,
    lengths_hbm, enrich_ref, maps_hbm, compliance_hbm, contact_hbm, loads_hbm, panel_hbm,
    solution_hbm, residual_hbm, violation_hbm,
    lengths_ref, maps_ref, compliance_ref, contact_ref, loads_ref,
    solution_ref, residual_ref, violation_ref, turned, panel, kept, kept_turned, onehot, diag, weights, direction, total, residual, violated, send, recv, bal_sums, space_sums, own_bal, own_space,
    input_sem, output_sem, send_sem, recv_sem, bal_send, bal_recv, space_send, space_recv,
):
    me_s = lax.axis_index("space")
    me_b = lax.axis_index("bal")
    rows, columns = panel.shape
    face_len = columns // FACES
    loads = loads_ref.shape[0]
    center, half_span, ratio_c = chebyshev_constants(columns, rows)

    inputs = (
        (maps_hbm, maps_ref), (lengths_hbm, lengths_ref), (loads_hbm, loads_ref), (panel_hbm, panel),
        (compliance_hbm, compliance_ref), (contact_hbm, contact_ref),
    )
    copies = [
        pltpu.make_async_copy(source, target, input_sem.at[index])
        for index, (source, target) in enumerate(inputs)
    ]
    for copy in copies:
        copy.start()

    barrier = pltpu.get_barrier_semaphore()
    for step in range(1, n_bal):
        pl.semaphore_signal(
            barrier, inc=1, device_id={"bal": lax.rem(me_b + step, n_bal)}, device_id_type=MESH
        )
    for step in range(1, n_space):
        pl.semaphore_signal(
            barrier, inc=1, device_id={"space": lax.rem(me_s + step, n_space)}, device_id_type=MESH
        )

    present = (me_s > 0, me_s < n_space - 1, me_b > 0, me_b < n_bal - 1)
    across = (
        {"space": jnp.maximum(me_s - 1, 0)},
        {"space": jnp.minimum(me_s + 1, n_space - 1)},
        {"bal": jnp.maximum(me_b - 1, 0)},
        {"bal": jnp.minimum(me_b + 1, n_bal - 1)},
    )
    part = loads // HALVES

    def face_copy(turn, half, face):
        return pltpu.make_async_remote_copy(
            src_ref=send.at[turn, half, face],
            dst_ref=recv.at[turn, half, face ^ 1],
            send_sem=send_sem.at[turn, half, face],
            recv_sem=recv_sem.at[turn, half, face ^ 1],
            device_id=across[face],
            device_id_type=MESH,
        )

    def start_face(turn, half, face):
        @pl.when(present[face])
        def _():
            face_copy(turn, half, face).start()

    def wait_face(turn, half, face):
        @pl.when(present[face])
        def _():
            face_copy(turn, half, face ^ 1).wait_recv()

    def lines(half):
        return slice(half * part, (half + 1) * part)

    def span(face):
        return slice(face * face_len, (face + 1) * face_len)

    copies[0].wait()
    copies[1].wait()
    row_of = lax.broadcasted_iota(jnp.int32, (face_len, face_len), 0)
    slot_of = lax.broadcasted_iota(jnp.int32, (face_len, face_len), 1)
    for pair in (SPACE_PAIR, BAL_PAIR):
        for face in pair:
            table = jnp.broadcast_to(maps_ref[face : face + 1, :], (face_len, face_len))
            hit = (row_of == table) & (slot_of < lengths_ref[0, face])
            onehot[face] = jnp.where(hit, 1.0, 0.0).astype(jnp.bfloat16)
        if pair == SPACE_PAIR:
            copies[2].wait()
        for face in pair:
            canonical = product(loads_ref[:, span(face)], onehot[face], CONTRACT_MIDDLE)
            for half in range(HALVES):
                send[0, half, face] = canonical[lines(half)]
        if pair == SPACE_PAIR:
            pl.semaphore_wait(barrier, n_bal - 1 + n_space - 1)
        for half in range(HALVES):
            for face in pair:
                start_face(0, half, face)

    def clear(turns):
        for face in range(FACES):
            @pl.when(jnp.logical_not(present[face]))
            def _():
                for turn in turns:
                    for half in range(HALVES):
                        recv[turn, half, face] = jnp.zeros((part, face_len), jnp.float32)

    clear((0,))

    lane = 128
    per_face = face_len // lane
    groups = columns // lane

    def prepare_weights():
        contact = contact_ref[...]
        group_rows = max(groups, 8)
        group_of = lax.broadcasted_iota(jnp.int32, (group_rows, contact.shape[1]), 0)
        place_of = lax.broadcasted_iota(jnp.int32, (lane, contact.shape[1]), 0)
        in_group = jnp.where(group_of == lax.shift_right_logical(contact, 7), 1.0, 0.0)
        at_place = jnp.where(place_of == (contact & (lane - 1)), 1.0, 0.0)
        counts = lax.dot_general(
            in_group.astype(jnp.bfloat16), at_place.astype(jnp.bfloat16), CONTRACT_LAST,
            preferred_element_type=jnp.float32,
        )
        for face in range(FACES):
            turned[face] = onehot[face].T
            weight = jnp.zeros((16, face_len), jnp.float32)
            for piece in range(per_face):
                group = face * per_face + piece
                row = jnp.broadcast_to(counts[group : group + 1, :], (16, lane)).astype(jnp.bfloat16)
                weight = weight + jnp.dot(
                    row, onehot[face, piece * lane : (piece + 1) * lane, :], preferred_element_type=jnp.float32
                )
            weights[:, span(face)] = weight

    for index in range(4, len(copies)):
        copies[index].wait()
    for face in range(FACES):
        wide = jnp.broadcast_to(compliance_ref[:, span(face)], (16, face_len))
        diag[:, span(face)] = product(wide, onehot[face], CONTRACT_MIDDLE, 3)

    copies[3].wait()
    live_rows = enrich_ref[0, 0] * BLOCK_ROWS
    keep = lax.broadcasted_iota(jnp.int32, (rows, face_len), 0) < live_rows
    for face in range(FACES):
        picked = jnp.dot(panel[:, span(face)], onehot[face], preferred_element_type=jnp.float32)
        masked = jnp.where(keep, picked, 0.0).astype(jnp.bfloat16)
        kept[:, span(face)] = masked
        kept_turned[span(face), :] = masked.T

    def pair_span(pair):
        return slice(pair[0] * face_len, (pair[-1] + 1) * face_len)

    def project(half, pair, running):
        term = jnp.dot(
            parts(direction[lines(half), pair_span(pair)], 2), kept_turned[pair_span(pair), :],
            preferred_element_type=jnp.float32,
        )
        return term if running is None else running + term

    def apply(turn, half, running):
        projected = parts(running[:part] + running[part:], 2)
        for pair in (SPACE_PAIR, BAL_PAIR):
            stacked = jnp.dot(projected, kept[:, pair_span(pair)], preferred_element_type=jnp.float32)
            image = (
                stacked[:part] + stacked[part:]
                + direction[lines(half), pair_span(pair)] * diag[0:1, pair_span(pair)]
            )
            for index, face in enumerate(pair):
                send[turn, half, face] = image[:, index * face_len : (index + 1) * face_len]
            for face in pair:
                start_face(turn, half, face)

    def share_violation():
        pieces = parts(violated[...], 3)
        ones = jnp.ones((16, lane), jnp.bfloat16)
        spread = lax.dot_general(ones, pieces, CONTRACT_LAST, preferred_element_type=jnp.float32)
        terms = spread[:8, :loads] + spread[:8, loads : 2 * loads] + spread[:8, 2 * loads :]
        own_bal[:, loads:] = jnp.zeros((8, own_bal.shape[1] - loads), jnp.float32)
        own_bal[:, :loads] = terms
        bal_sums[me_b] = own_bal[...]
        for step in range(1, n_bal):
            pltpu.make_async_remote_copy(
                src_ref=own_bal, dst_ref=bal_sums.at[me_b],
                send_sem=bal_send.at[step], recv_sem=bal_recv.at[step],
                device_id={"bal": lax.rem(me_b + step, n_bal)}, device_id_type=MESH,
            ).start()

    for half in range(HALVES):
        running = None
        for pair in (BAL_PAIR, SPACE_PAIR):
            for face in pair:
                wait_face(0, half, face)
            for face in pair:
                first = send[0, half, face] + recv[0, half, face]
                residual[lines(half), span(face)] = first
                direction[lines(half), span(face)] = first * (1.0 / center)
                total[lines(half), span(face)] = first * (1.0 / center)
            running = project(half, pair, running)
        apply(1, half, running)

    clear(range(1, ITERS + 1))
    prepare_weights()

    cheb_rho = 1.0 / ratio_c
    for turn in range(1, ITERS):
        rho_next = 1.0 / (2.0 * ratio_c - cheb_rho)
        for half in range(HALVES):
            running = None
            weighted = jnp.zeros((part, face_len), jnp.float32)
            for pair in (BAL_PAIR, SPACE_PAIR):
                for face in pair:
                    wait_face(turn, half, face)
                for face in pair:
                    updated = residual[lines(half), span(face)] - (send[turn, half, face] + recv[turn, half, face])
                    residual[lines(half), span(face)] = updated
                    moved = (
                        rho_next * cheb_rho * direction[lines(half), span(face)]
                        + 2.0 * rho_next / half_span * updated
                    )
                    direction[lines(half), span(face)] = moved
                    summed = total[lines(half), span(face)] + moved
                    total[lines(half), span(face)] = summed
                    negative = jnp.minimum(summed, 0.0)
                    weighted = weighted + negative * negative * weights[0:1, span(face)]
                running = project(half, pair, running)
            if turn + 1 == ITERS:
                narrow = weighted[:, :lane]
                for piece in range(1, per_face):
                    narrow = narrow + weighted[:, piece * lane : (piece + 1) * lane]
                violated[lines(half), :] = narrow
                if half + 1 == HALVES:
                    share_violation()
            apply(turn + 1, half, running)
        cheb_rho = rho_next

    for face in range(FACES):
        solution_ref[:, span(face)] = product(total[:, span(face)], turned[face], CONTRACT_MIDDLE)
    solution_copy = pltpu.make_async_copy(solution_ref, solution_hbm, output_sem.at[0])
    solution_copy.start()

    def settle(half):
        for pair in (BAL_PAIR, SPACE_PAIR):
            for face in pair:
                wait_face(ITERS, half, face)
            for face in pair:
                final = residual[lines(half), span(face)] - (send[ITERS, half, face] + recv[ITERS, half, face])
                residual_ref[lines(half), span(face)] = product(final, turned[face], CONTRACT_MIDDLE)
        copy = pltpu.make_async_copy(
            residual_ref.at[lines(half)], residual_hbm.at[lines(half)], output_sem.at[2 + half]
        )
        copy.start()
        return copy


    for step in range(1, n_bal):
        source = lax.rem(me_b + n_bal - step, n_bal)
        pltpu.make_async_remote_copy(
            src_ref=own_bal, dst_ref=bal_sums.at[source],
            send_sem=bal_send.at[step], recv_sem=bal_recv.at[step],
            device_id={"bal": source}, device_id_type=MESH,
        ).wait()
    summed = bal_sums[0]
    for index in range(1, n_bal):
        summed = summed + bal_sums[index]
    own_space[...] = summed
    space_sums[me_s] = summed
    for step in range(1, n_space):
        pltpu.make_async_remote_copy(
            src_ref=own_space, dst_ref=space_sums.at[me_s],
            send_sem=space_send.at[step], recv_sem=space_recv.at[step],
            device_id={"space": lax.rem(me_s + step, n_space)}, device_id_type=MESH,
        ).start()

    residual_copies = [settle(half) for half in range(HALVES)]

    for step in range(1, n_space):
        source = lax.rem(me_s + n_space - step, n_space)
        pltpu.make_async_remote_copy(
            src_ref=own_space, dst_ref=space_sums.at[source],
            send_sem=space_send.at[step], recv_sem=space_recv.at[step],
            device_id={"space": source}, device_id_type=MESH,
        ).wait()
    summed = space_sums[0]
    for index in range(1, n_space):
        summed = summed + space_sums[index]
    violation_ref[...] = jnp.sqrt(summed[0:1, :loads] + 1e-06)
    violation_copy = pltpu.make_async_copy(violation_ref, violation_hbm, output_sem.at[1])
    violation_copy.start()

    for turn in range(ITERS + 1):
        for face in range(FACES):
            @pl.when(present[face])
            def _():
                for half in range(HALVES):
                    face_copy(turn, half, face).wait_send()
    solution_copy.wait()
    violation_copy.wait()
    for copy in residual_copies:
        copy.wait()


def finish(
    solution_in, residual_in, violation_in, solution_out, residual_out, violation_out,
    solution_held, residual_held, violation_held, in_sems, out_sems,
):
    rows = solution_held.shape[0]
    part = rows // HALVES
    moves = [(violation_in, violation_held, violation_out)]
    for half in range(HALVES):
        span = slice(half * part, (half + 1) * part)
        moves.append((residual_in.at[span], residual_held.at[span], residual_out.at[span]))
        moves.append((solution_in.at[span], solution_held.at[span], solution_out.at[span]))
    fetches = [
        pltpu.make_async_copy(source, held, in_sems.at[index]) for index, (source, held, _) in enumerate(moves)
    ]
    stores = [
        pltpu.make_async_copy(held, target, out_sems.at[index]) for index, (_, held, target) in enumerate(moves)
    ]
    for fetch in fetches:
        fetch.start()
    for fetch, store in zip(fetches, stores):
        fetch.wait()
        store.start()
    for store in stores:
        store.wait()


def local(n_space, n_bal, panels, enrich, compliance, loads, face_maps, face_lengths, contact):
    rows, columns = panels.shape[2:]
    n_loads = loads.shape[2]
    face_len = columns // FACES
    width = -(-n_loads // 128) * 128
    hbm = pl.BlockSpec(memory_space=pltpu.HBM)
    turns = ITERS + 1
    flops = 2 * rows * columns * (face_len + ITERS * 4 * n_loads)
    field = (n_loads, columns)
    out = pl.pallas_call(
        functools.partial(kernel, n_space, n_bal),
        out_shape=(
            jax.ShapeDtypeStruct(field, jnp.float32),
            jax.ShapeDtypeStruct(field, jnp.float32),
            jax.ShapeDtypeStruct((1, n_loads), jnp.float32),
        ),
        in_specs=[hbm, pl.BlockSpec(memory_space=pltpu.SMEM)] + [hbm] * 5,
        out_specs=(hbm, hbm, hbm),
        scratch_shapes=[
            pltpu.SMEM((1, FACES), jnp.int32),
            pltpu.VMEM((FACES, face_len), jnp.int32),
            pltpu.VMEM((1, columns), jnp.float32),
            pltpu.VMEM((1, contact.shape[2]), jnp.int32),
            pltpu.VMEM(field, jnp.float32),
            pltpu.VMEM(field, jnp.float32),
            pltpu.VMEM(field, jnp.float32),
            pltpu.VMEM((1, n_loads), jnp.float32),
            pltpu.VMEM((FACES, face_len, face_len), jnp.bfloat16),
            pltpu.VMEM((rows, columns), jnp.bfloat16),
            pltpu.VMEM((rows, columns), jnp.bfloat16),
            pltpu.VMEM((rows, columns), jnp.bfloat16),
            pltpu.VMEM((FACES, face_len, face_len), jnp.bfloat16),
            pltpu.VMEM((16, columns), jnp.float32),
            pltpu.VMEM((16, columns), jnp.float32),
            pltpu.VMEM(field, jnp.float32),
            pltpu.VMEM(field, jnp.float32),
            pltpu.VMEM(field, jnp.float32),
            pltpu.VMEM((n_loads, 128), jnp.float32),
            pltpu.VMEM((turns, HALVES, FACES, n_loads // HALVES, face_len), jnp.float32),
            pltpu.VMEM((turns, HALVES, FACES, n_loads // HALVES, face_len), jnp.float32),
            pltpu.VMEM((n_bal, 8, width), jnp.float32),
            pltpu.VMEM((n_space, 8, width), jnp.float32),
            pltpu.VMEM((8, width), jnp.float32),
            pltpu.VMEM((8, width), jnp.float32),
            pltpu.SemaphoreType.DMA((6,)),
            pltpu.SemaphoreType.DMA((2 + HALVES,)),
            pltpu.SemaphoreType.DMA((turns, HALVES, FACES)),
            pltpu.SemaphoreType.DMA((turns, HALVES, FACES)),
            pltpu.SemaphoreType.DMA((n_bal,)),
            pltpu.SemaphoreType.DMA((n_bal,)),
            pltpu.SemaphoreType.DMA((n_space,)),
            pltpu.SemaphoreType.DMA((n_space,)),
        ],
        compiler_params=pltpu.CompilerParams(
            collective_id=0, has_side_effects=True, vmem_limit_bytes=VMEM_BYTES
        ),
        cost_estimate=pl.CostEstimate(
            flops=flops, bytes_accessed=2 * rows * columns + 12 * n_loads * columns, transcendentals=n_loads
        ),
        name="feti",
    )(
        face_lengths[0], enrich, face_maps[0, 0], compliance[0], contact[0], loads[0, 0], panels[0, 0]
    )
    finished = pl.pallas_call(
        finish,
        out_shape=(
            jax.ShapeDtypeStruct(field, jnp.float32),
            jax.ShapeDtypeStruct(field, jnp.float32),
            jax.ShapeDtypeStruct((1, n_loads), jnp.float32),
        ),
        in_specs=[hbm] * 3,
        out_specs=(hbm, hbm, hbm),
        scratch_shapes=[
            pltpu.VMEM(field, jnp.float32),
            pltpu.VMEM(field, jnp.float32),
            pltpu.VMEM((1, n_loads), jnp.float32),
            pltpu.SemaphoreType.DMA((1 + 2 * HALVES,)),
            pltpu.SemaphoreType.DMA((1 + 2 * HALVES,)),
        ],
        compiler_params=pltpu.CompilerParams(vmem_limit_bytes=VMEM_BYTES),
        name="finish",
    )(*out)
    return (finished[0][None, None], finished[1][None, None], finished[2][0])


def solution(mesh):
    in_specs = (
        P("space", "bal", None, None),
        P("space", "bal"),
        P("space", "bal", None),
        P("space", "bal", None, None),
        P("space", "bal", None, None),
        P("space", "bal", None),
        P("space", "bal", None),
    )
    out_specs = (P("space", "bal", None, None), P("space", "bal", None, None), P())
    body = functools.partial(local, mesh.shape["space"], mesh.shape["bal"])
    return jax.shard_map(body, mesh=mesh, in_specs=in_specs, out_specs=out_specs, check_vma=False)
```

```python
import functools
import math

import jax
import jax.numpy as jnp
from jax import lax
from jax.experimental import pallas as pl
from jax.experimental.pallas import tpu as pltpu
from jax.sharding import PartitionSpec as P

BLOCK_ROWS = 512
ITERS = 3
FACES = 4
HALVES = 1
VMEM_BYTES = 64 * 1024 * 1024
SPACE_PAIR = (0, 1)
BAL_PAIR = (2, 3)
MESH = pl.DeviceIdType.MESH
CONTRACT_LAST = (((1,), (1,)), ((), ()))
CONTRACT_MIDDLE = (((1,), (0,)), ((), ()))


def chebyshev_constants(iface, rows):
    upper = 2.6 * (1.0 + math.sqrt(iface / rows)) ** 2 + 4.0
    lower = 0.5
    center = (upper + lower) / 2.0
    half_span = (upper - lower) / 2.0
    return (center, half_span, center / half_span)


def parts(value, count):
    taken = []
    rest = value
    for index in range(count):
        part = rest.astype(jnp.bfloat16)
        taken.append(part)
        if index + 1 < count:
            rest = rest - part.astype(jnp.float32)
    return jnp.concatenate(taken, axis=0)


def product(value, matrix, dims, count=2):
    rows = value.shape[0]
    stacked = lax.dot_general(
        parts(value, count), matrix, dims, preferred_element_type=jnp.float32
    )
    total = stacked[:rows]
    for index in range(1, count):
        total = total + stacked[index * rows : (index + 1) * rows]
    return total


def kernel(
    n_space, n_bal,
    lengths_hbm, enrich_ref, maps_hbm, compliance_hbm, contact_hbm, loads_hbm, panel_hbm,
    solution_hbm, residual_hbm, violation_hbm,
    lengths_ref, maps_ref, compliance_ref, contact_ref, loads_ref,
    solution_ref, residual_ref, violation_ref, turned, panel, kept, kept_turned, gram_high, gram_low, onehot, diag, weights, direction, total, residual, violated, send, recv, bal_sums, space_sums, own_bal, own_space,
    input_sem, output_sem, send_sem, recv_sem, bal_send, bal_recv, space_send, space_recv,
):
    me_s = lax.axis_index("space")
    me_b = lax.axis_index("bal")
    rows, columns = panel.shape
    face_len = columns // FACES
    loads = loads_ref.shape[0]
    center, half_span, ratio_c = chebyshev_constants(columns, rows)

    inputs = (
        (maps_hbm, maps_ref), (lengths_hbm, lengths_ref), (loads_hbm, loads_ref), (panel_hbm, panel),
        (compliance_hbm, compliance_ref), (contact_hbm, contact_ref),
    )
    copies = [
        pltpu.make_async_copy(source, target, input_sem.at[index])
        for index, (source, target) in enumerate(inputs)
    ]
    for copy in copies:
        copy.start()

    barrier = pltpu.get_barrier_semaphore()
    for step in range(1, n_bal):
        pl.semaphore_signal(
            barrier, inc=1, device_id={"bal": lax.rem(me_b + step, n_bal)}, device_id_type=MESH
        )
    for step in range(1, n_space):
        pl.semaphore_signal(
            barrier, inc=1, device_id={"space": lax.rem(me_s + step, n_space)}, device_id_type=MESH
        )

    present = (me_s > 0, me_s < n_space - 1, me_b > 0, me_b < n_bal - 1)
    across = (
        {"space": jnp.maximum(me_s - 1, 0)},
        {"space": jnp.minimum(me_s + 1, n_space - 1)},
        {"bal": jnp.maximum(me_b - 1, 0)},
        {"bal": jnp.minimum(me_b + 1, n_bal - 1)},
    )
    part = loads // HALVES

    def face_copy(turn, half, face):
        return pltpu.make_async_remote_copy(
            src_ref=send.at[turn, half, face],
            dst_ref=recv.at[turn, half, face ^ 1],
            send_sem=send_sem.at[turn, half, face],
            recv_sem=recv_sem.at[turn, half, face ^ 1],
            device_id=across[face],
            device_id_type=MESH,
        )

    def start_face(turn, half, face):
        @pl.when(present[face])
        def _():
            face_copy(turn, half, face).start()

    def wait_face(turn, half, face):
        @pl.when(present[face])
        def _():
            face_copy(turn, half, face ^ 1).wait_recv()

    def lines(half):
        return slice(half * part, (half + 1) * part)

    def span(face):
        return slice(face * face_len, (face + 1) * face_len)

    copies[0].wait()
    copies[1].wait()
    row_of = lax.broadcasted_iota(jnp.int32, (face_len, face_len), 0)
    slot_of = lax.broadcasted_iota(jnp.int32, (face_len, face_len), 1)
    for pair in (SPACE_PAIR, BAL_PAIR):
        for face in pair:
            table = jnp.broadcast_to(maps_ref[face : face + 1, :], (face_len, face_len))
            hit = (row_of == table) & (slot_of < lengths_ref[0, face])
            onehot[face] = jnp.where(hit, 1.0, 0.0).astype(jnp.bfloat16)
        if pair == SPACE_PAIR:
            copies[2].wait()
        for face in pair:
            canonical = product(loads_ref[:, span(face)], onehot[face], CONTRACT_MIDDLE)
            for half in range(HALVES):
                send[0, half, face] = canonical[lines(half)]
        if pair == SPACE_PAIR:
            pl.semaphore_wait(barrier, n_bal - 1 + n_space - 1)
        for half in range(HALVES):
            for face in pair:
                start_face(0, half, face)

    def clear(turns):
        for face in range(FACES):
            @pl.when(jnp.logical_not(present[face]))
            def _():
                for turn in turns:
                    for half in range(HALVES):
                        recv[turn, half, face] = jnp.zeros((part, face_len), jnp.float32)

    clear((0,))

    lane = 128
    per_face = face_len // lane
    groups = columns // lane

    def prepare_weights():
        contact = contact_ref[...]
        group_rows = max(groups, 8)
        group_of = lax.broadcasted_iota(jnp.int32, (group_rows, contact.shape[1]), 0)
        place_of = lax.broadcasted_iota(jnp.int32, (lane, contact.shape[1]), 0)
        in_group = jnp.where(group_of == lax.shift_right_logical(contact, 7), 1.0, 0.0)
        at_place = jnp.where(place_of == (contact & (lane - 1)), 1.0, 0.0)
        counts = lax.dot_general(
            in_group.astype(jnp.bfloat16), at_place.astype(jnp.bfloat16), CONTRACT_LAST,
            preferred_element_type=jnp.float32,
        )
        for face in range(FACES):
            turned[face] = onehot[face].T
            weight = jnp.zeros((16, face_len), jnp.float32)
            for piece in range(per_face):
                group = face * per_face + piece
                row = jnp.broadcast_to(counts[group : group + 1, :], (16, lane)).astype(jnp.bfloat16)
                weight = weight + jnp.dot(
                    row, onehot[face, piece * lane : (piece + 1) * lane, :], preferred_element_type=jnp.float32
                )
            weights[:, span(face)] = weight

    for index in range(4, len(copies)):
        copies[index].wait()
    for face in range(FACES):
        wide = jnp.broadcast_to(compliance_ref[:, span(face)], (16, face_len))
        diag[:, span(face)] = product(wide, onehot[face], CONTRACT_MIDDLE, 3)

    copies[3].wait()
    live_rows = enrich_ref[0, 0] * BLOCK_ROWS
    keep = lax.broadcasted_iota(jnp.int32, (rows, face_len), 0) < live_rows
    for face in range(FACES):
        picked = jnp.dot(panel[:, span(face)], onehot[face], preferred_element_type=jnp.float32)
        masked = jnp.where(keep, picked, 0.0).astype(jnp.bfloat16)
        kept[:, span(face)] = masked
        kept_turned[span(face), :] = masked.T

    def pair_span(pair):
        return slice(pair[0] * face_len, (pair[-1] + 1) * face_len)

    def project(half, pair, running):
        term = jnp.dot(
            parts(direction[lines(half), pair_span(pair)], 2), kept_turned[pair_span(pair), :],
            preferred_element_type=jnp.float32,
        )
        return term if running is None else running + term

    def apply(turn, half, running):
        projected = parts(running[:part] + running[part:], 2)
        for pair in (SPACE_PAIR, BAL_PAIR):
            stacked = jnp.dot(projected, kept[:, pair_span(pair)], preferred_element_type=jnp.float32)
            image = (
                stacked[:part] + stacked[part:]
                + direction[lines(half), pair_span(pair)] * diag[0:1, pair_span(pair)]
            )
            for index, face in enumerate(pair):
                send[turn, half, face] = image[:, index * face_len : (index + 1) * face_len]
            for face in pair:
                start_face(turn, half, face)

    def share_violation():
        pieces = parts(violated[...], 3)
        ones = jnp.ones((16, lane), jnp.bfloat16)
        spread = lax.dot_general(ones, pieces, CONTRACT_LAST, preferred_element_type=jnp.float32)
        terms = spread[:8, :loads] + spread[:8, loads : 2 * loads] + spread[:8, 2 * loads :]
        own_bal[:, loads:] = jnp.zeros((8, own_bal.shape[1] - loads), jnp.float32)
        own_bal[:, :loads] = terms
        bal_sums[me_b] = own_bal[...]
        for step in range(1, n_bal):
            pltpu.make_async_remote_copy(
                src_ref=own_bal, dst_ref=bal_sums.at[me_b],
                send_sem=bal_send.at[step], recv_sem=bal_recv.at[step],
                device_id={"bal": lax.rem(me_b + step, n_bal)}, device_id_type=MESH,
            ).start()

    for half in range(HALVES):
        running = None
        for pair in (BAL_PAIR, SPACE_PAIR):
            for face in pair:
                wait_face(0, half, face)
            for face in pair:
                first = send[0, half, face] + recv[0, half, face]
                residual[lines(half), span(face)] = first
                direction[lines(half), span(face)] = first * (1.0 / center)
                total[lines(half), span(face)] = first * (1.0 / center)
            running = project(half, pair, running)
        apply(1, half, running)

    clear(range(1, ITERS + 1))

    for face in range(FACES):
        gram = jnp.dot(kept_turned[...], kept[:, span(face)], preferred_element_type=jnp.float32)
        high = gram.astype(jnp.bfloat16)
        gram_high[:, span(face)] = high
        gram_low[:, span(face)] = (gram - high.astype(jnp.float32)).astype(jnp.bfloat16)

    def multiply(half, pair, running):
        stacked = parts(direction[lines(half), pair_span(pair)], 2)
        term = jnp.dot(stacked, gram_high[pair_span(pair), :], preferred_element_type=jnp.float32)
        small = jnp.dot(stacked[:part], gram_low[pair_span(pair), :], preferred_element_type=jnp.float32)
        term = term[:part] + term[part:] + small
        return term if running is None else running + term

    def send_image(turn, half, product_rows):
        image = product_rows + direction[lines(half), :] * diag[0:1, :]
        for face in range(FACES):
            send[turn, half, face] = image[:, span(face)]
        for face in SPACE_PAIR + BAL_PAIR:
            start_face(turn, half, face)

    cheb_rho = 1.0 / ratio_c
    for turn in range(1, ITERS):
        rho_next = 1.0 / (2.0 * ratio_c - cheb_rho)
        for half in range(HALVES):
            running = None
            weighted = jnp.zeros((part, face_len), jnp.float32)
            for pair in (BAL_PAIR, SPACE_PAIR):
                for face in pair:
                    wait_face(turn, half, face)
                for face in pair:
                    updated = residual[lines(half), span(face)] - (send[turn, half, face] + recv[turn, half, face])
                    residual[lines(half), span(face)] = updated
                    moved = (
                        rho_next * cheb_rho * direction[lines(half), span(face)]
                        + 2.0 * rho_next / half_span * updated
                    )
                    direction[lines(half), span(face)] = moved
                    summed = total[lines(half), span(face)] + moved
                    total[lines(half), span(face)] = summed
                    negative = jnp.minimum(summed, 0.0)
                    weighted = weighted + negative * negative * weights[0:1, span(face)]
                running = multiply(half, pair, running)
            if turn + 1 == ITERS:
                narrow = weighted[:, :lane]
                for piece in range(1, per_face):
                    narrow = narrow + weighted[:, piece * lane : (piece + 1) * lane]
                violated[lines(half), :] = narrow
                if half + 1 == HALVES:
                    share_violation()
            send_image(turn + 1, half, running)
        if turn == 1:
            prepare_weights()
        cheb_rho = rho_next

    for face in range(FACES):
        solution_ref[:, span(face)] = product(total[:, span(face)], turned[face], CONTRACT_MIDDLE)
    solution_copy = pltpu.make_async_copy(solution_ref, solution_hbm, output_sem.at[0])
    solution_copy.start()

    def settle(half):
        for pair in (BAL_PAIR, SPACE_PAIR):
            for face in pair:
                wait_face(ITERS, half, face)
            for face in pair:
                final = residual[lines(half), span(face)] - (send[ITERS, half, face] + recv[ITERS, half, face])
                residual_ref[lines(half), span(face)] = product(final, turned[face], CONTRACT_MIDDLE)
        copy = pltpu.make_async_copy(
            residual_ref.at[lines(half)], residual_hbm.at[lines(half)], output_sem.at[2 + half]
        )
        copy.start()
        return copy


    for step in range(1, n_bal):
        source = lax.rem(me_b + n_bal - step, n_bal)
        pltpu.make_async_remote_copy(
            src_ref=own_bal, dst_ref=bal_sums.at[source],
            send_sem=bal_send.at[step], recv_sem=bal_recv.at[step],
            device_id={"bal": source}, device_id_type=MESH,
        ).wait()
    summed = bal_sums[0]
    for index in range(1, n_bal):
        summed = summed + bal_sums[index]
    own_space[...] = summed
    space_sums[me_s] = summed
    for step in range(1, n_space):
        pltpu.make_async_remote_copy(
            src_ref=own_space, dst_ref=space_sums.at[me_s],
            send_sem=space_send.at[step], recv_sem=space_recv.at[step],
            device_id={"space": lax.rem(me_s + step, n_space)}, device_id_type=MESH,
        ).start()

    residual_copies = [settle(half) for half in range(HALVES)]

    for step in range(1, n_space):
        source = lax.rem(me_s + n_space - step, n_space)
        pltpu.make_async_remote_copy(
            src_ref=own_space, dst_ref=space_sums.at[source],
            send_sem=space_send.at[step], recv_sem=space_recv.at[step],
            device_id={"space": source}, device_id_type=MESH,
        ).wait()
    summed = space_sums[0]
    for index in range(1, n_space):
        summed = summed + space_sums[index]
    violation_ref[...] = jnp.sqrt(summed[0:1, :loads] + 1e-06)
    violation_copy = pltpu.make_async_copy(violation_ref, violation_hbm, output_sem.at[1])
    violation_copy.start()

    for turn in range(ITERS + 1):
        for face in range(FACES):
            @pl.when(present[face])
            def _():
                for half in range(HALVES):
                    face_copy(turn, half, face).wait_send()
    solution_copy.wait()
    violation_copy.wait()
    for copy in residual_copies:
        copy.wait()


def finish(
    solution_in, residual_in, violation_in, solution_out, residual_out, violation_out,
    solution_held, residual_held, violation_held, in_sems, out_sems,
):
    rows = solution_held.shape[0]
    part = rows // HALVES
    moves = [(violation_in, violation_held, violation_out)]
    for half in range(HALVES):
        span = slice(half * part, (half + 1) * part)
        moves.append((residual_in.at[span], residual_held.at[span], residual_out.at[span]))
        moves.append((solution_in.at[span], solution_held.at[span], solution_out.at[span]))
    fetches = [
        pltpu.make_async_copy(source, held, in_sems.at[index]) for index, (source, held, _) in enumerate(moves)
    ]
    stores = [
        pltpu.make_async_copy(held, target, out_sems.at[index]) for index, (_, held, target) in enumerate(moves)
    ]
    for fetch in fetches:
        fetch.start()
    for fetch, store in zip(fetches, stores):
        fetch.wait()
        store.start()
    for store in stores:
        store.wait()


def local(n_space, n_bal, panels, enrich, compliance, loads, face_maps, face_lengths, contact):
    rows, columns = panels.shape[2:]
    n_loads = loads.shape[2]
    face_len = columns // FACES
    width = -(-n_loads // 128) * 128
    hbm = pl.BlockSpec(memory_space=pltpu.HBM)
    turns = ITERS + 1
    flops = 2 * rows * columns * (face_len + ITERS * 4 * n_loads)
    field = (n_loads, columns)
    out = pl.pallas_call(
        functools.partial(kernel, n_space, n_bal),
        out_shape=(
            jax.ShapeDtypeStruct(field, jnp.float32),
            jax.ShapeDtypeStruct(field, jnp.float32),
            jax.ShapeDtypeStruct((1, n_loads), jnp.float32),
        ),
        in_specs=[hbm, pl.BlockSpec(memory_space=pltpu.SMEM)] + [hbm] * 5,
        out_specs=(hbm, hbm, hbm),
        scratch_shapes=[
            pltpu.SMEM((1, FACES), jnp.int32),
            pltpu.VMEM((FACES, face_len), jnp.int32),
            pltpu.VMEM((1, columns), jnp.float32),
            pltpu.VMEM((1, contact.shape[2]), jnp.int32),
            pltpu.VMEM(field, jnp.float32),
            pltpu.VMEM(field, jnp.float32),
            pltpu.VMEM(field, jnp.float32),
            pltpu.VMEM((1, n_loads), jnp.float32),
            pltpu.VMEM((FACES, face_len, face_len), jnp.bfloat16),
            pltpu.VMEM((rows, columns), jnp.bfloat16),
            pltpu.VMEM((rows, columns), jnp.bfloat16),
            pltpu.VMEM((columns, rows), jnp.bfloat16),
            pltpu.VMEM((columns, columns), jnp.bfloat16),
            pltpu.VMEM((columns, columns), jnp.bfloat16),
            pltpu.VMEM((FACES, face_len, face_len), jnp.bfloat16),
            pltpu.VMEM((16, columns), jnp.float32),
            pltpu.VMEM((16, columns), jnp.float32),
            pltpu.VMEM(field, jnp.float32),
            pltpu.VMEM(field, jnp.float32),
            pltpu.VMEM(field, jnp.float32),
            pltpu.VMEM((n_loads, 128), jnp.float32),
            pltpu.VMEM((turns, HALVES, FACES, n_loads // HALVES, face_len), jnp.float32),
            pltpu.VMEM((turns, HALVES, FACES, n_loads // HALVES, face_len), jnp.float32),
            pltpu.VMEM((n_bal, 8, width), jnp.float32),
            pltpu.VMEM((n_space, 8, width), jnp.float32),
            pltpu.VMEM((8, width), jnp.float32),
            pltpu.VMEM((8, width), jnp.float32),
            pltpu.SemaphoreType.DMA((6,)),
            pltpu.SemaphoreType.DMA((2 + HALVES,)),
            pltpu.SemaphoreType.DMA((turns, HALVES, FACES)),
            pltpu.SemaphoreType.DMA((turns, HALVES, FACES)),
            pltpu.SemaphoreType.DMA((n_bal,)),
            pltpu.SemaphoreType.DMA((n_bal,)),
            pltpu.SemaphoreType.DMA((n_space,)),
            pltpu.SemaphoreType.DMA((n_space,)),
        ],
        compiler_params=pltpu.CompilerParams(
            collective_id=0, has_side_effects=True, vmem_limit_bytes=VMEM_BYTES
        ),
        cost_estimate=pl.CostEstimate(
            flops=flops, bytes_accessed=2 * rows * columns + 12 * n_loads * columns, transcendentals=n_loads
        ),
        name="feti",
    )(
        face_lengths[0], enrich, face_maps[0, 0], compliance[0], contact[0], loads[0, 0], panels[0, 0]
    )
    finished = pl.pallas_call(
        finish,
        out_shape=(
            jax.ShapeDtypeStruct(field, jnp.float32),
            jax.ShapeDtypeStruct(field, jnp.float32),
            jax.ShapeDtypeStruct((1, n_loads), jnp.float32),
        ),
        in_specs=[hbm] * 3,
        out_specs=(hbm, hbm, hbm),
        scratch_shapes=[
            pltpu.VMEM(field, jnp.float32),
            pltpu.VMEM(field, jnp.float32),
            pltpu.VMEM((1, n_loads), jnp.float32),
            pltpu.SemaphoreType.DMA((1 + 2 * HALVES,)),
            pltpu.SemaphoreType.DMA((1 + 2 * HALVES,)),
        ],
        compiler_params=pltpu.CompilerParams(vmem_limit_bytes=VMEM_BYTES),
        name="finish",
    )(*out)
    return (finished[0][None, None], finished[1][None, None], finished[2][0])


def solution(mesh):
    in_specs = (
        P("space", "bal", None, None),
        P("space", "bal"),
        P("space", "bal", None),
        P("space", "bal", None, None),
        P("space", "bal", None, None),
        P("space", "bal", None),
        P("space", "bal", None),
    )
    out_specs = (P("space", "bal", None, None), P("space", "bal", None, None), P())
    body = functools.partial(local, mesh.shape["space"], mesh.shape["bal"])
    return jax.shard_map(body, mesh=mesh, in_specs=in_specs, out_specs=out_specs, check_vma=False)
```
